512 devices in a mesh: tm: 32 (over y, z_lo, core), rows: 16 (over z_hi, x).
Axes of the slice: x: 4, y: 4, z: 16 (z_hi: 4, z_lo: 4; z = z_hi * 4 + z_lo), core: 2. Of those that a mesh axis runs over, the one named last changes fastest.
Arguments:
- latent_features: bfloat16 [64, 16, 160, 384], P('tm', 'rows'), may hold values from -6 to 6
- attn_gain: float32 [384], replicated, may hold values from 0.1 to 1.9
- w_query: bfloat16 [384, 384], replicated
- w_key: bfloat16 [384, 384], replicated, may hold values from -0.3125 to 0.3125
- w_value: bfloat16 [384, 384], replicated, may hold values from -0.3125 to 0.3125
- w_proj: bfloat16 [384, 384], replicated, may hold values from -0.3125 to 0.3125
- unit_gain: float32 [384], replicated, may hold values from 0.1 to 1.9
- conv_weight: bfloat16 [3, 3, 3, 384, 384], P(None, None, None, 'rows'), may hold values from -0.0625 to 0.0625
- upsample_weight: bfloat16 [3, 384, 768], replicated, may hold values from -0.1875 to 0.1875
Outputs:
- upsampled: bfloat16 [128, 16, 160, 384], P('tm', 'rows')
The draws below stay inside these ranges and needn't reach their ends.
All inputs are finite; a program needn't handle non-finite values.
Results may differ from the reference program's by a relative error of at most 0.015.
The reference program's roundings to bfloat16 on the way (of `normed`, `queries`, `attn_mixed`, `attended`, `activated` and `unit_out`) count: a program that leaves them out, or rounds other values in their place, can miss the bound.
Values may be sent and summed in bfloat16 or wider, within the bound.
A program may use at most 64 MiB of HBM per device.

```python
import math
import jax
import jax.numpy as jnp
from jax import lax

C = 384
W = 160
FRAMES = 64
ROWS = 16


def draw_w_query(key, part):
    key = jax.random.fold_in(key, 5)
    drawn = jax.random.normal(key, (C, C), jnp.float32) * C ** (-0.5)
    drawn = drawn * 4.0
    return drawn.astype(jnp.bfloat16)


def levels(key, extent, pieces, smallest, top_value):
    loudness, own = 1.0, jax.random.fold_in(key, 6)
    for position, blocks in pieces:
        draws = jnp.exp(jax.random.uniform(jax.random.fold_in(own, position), (blocks,), jnp.float32, smallest / len(pieces), top_value / len(pieces)))
        loudness = loudness * jnp.repeat(draws, extent[position] // blocks).reshape([-1 if axis == position else 1 for axis in range(len(extent))])
    return loudness


def normal_values(stream_key, shape, deviation, most, cuts=(), dtype=jnp.bfloat16):
    level = levels(stream_key, shape, cuts, -0.22, 0.18) if cuts else 1.0
    result = jax.random.normal(stream_key, shape, jnp.float32) * deviation * level
    return jnp.minimum(jnp.maximum(result, -most), most).astype(dtype)


def setup_inputs(seed: int = 0) -> dict:
    arg_keys = jax.random.split(jax.random.key(seed), 10)
    latent_features = normal_values(arg_keys[0], (FRAMES, ROWS, W, C), 1.0, 6.0, ((0, 32), (1, 16)))
    attn_gain = jnp.clip(1.0 + 0.18 * jax.random.normal(arg_keys[1], (C,), jnp.float32), 0.1, 1.9)
    w_query = draw_w_query(jax.random.fold_in(arg_keys[9], 71), 0)
    w_key = normal_values(arg_keys[3], (C, C), C ** -0.5, 0.3125)
    w_value = normal_values(arg_keys[4], (C, C), C ** -0.5, 0.3125)
    w_proj = normal_values(arg_keys[5], (C, C), C ** -0.5, 0.3125)
    unit_gain = jnp.clip(1.0 + 0.18 * jax.random.normal(arg_keys[6], (C,), jnp.float32), 0.1, 1.9)
    conv_weight = normal_values(arg_keys[7], (3, 3, 3, C, C), (27 * C) ** -0.5, 0.0625, ((3, 16),))
    upsample_weight = normal_values(arg_keys[8], (3, C, 2 * C), (3 * C) ** -0.5, 0.1875)
    return dict(latent_features=latent_features, attn_gain=attn_gain, w_query=w_query, w_key=w_key, w_value=w_value, w_proj=w_proj, unit_gain=unit_gain, conv_weight=conv_weight, upsample_weight=upsample_weight)


epsilon = 1e-06

def rms_scale(values, gain):
    widened = values.astype(jnp.float32)
    return widened * lax.rsqrt(lax.optimization_barrier(jnp.mean(widened * widened, axis=-1, keepdims=True)) + epsilon) * gain

def volume_conv(extended, kernel, padding):
    return lax.conv_general_dilated(extended[None], kernel, (1, 1, 1), padding, dimension_numbers=('NDHWC', 'DHWIO', 'NDHWC'), preferred_element_type=jnp.float32)[0]

def time_conv(extended, kernel):
    frames = extended.shape[0] - 2
    stretched = jnp.dot(extended[0:frames], kernel[0], preferred_element_type=jnp.float32)
    stretched = stretched + jnp.dot(extended[1:frames + 1], kernel[1], preferred_element_type=jnp.float32)
    stretched = stretched + jnp.dot(extended[2:frames + 2], kernel[2], preferred_element_type=jnp.float32)
    return stretched

def alternate(stretched):
    frames, rows_here, columns, doubled = stretched.shape
    channels = doubled // 2
    split_up = stretched.reshape(frames, rows_here, columns, 2, channels)
    split_up = jnp.transpose(split_up, (0, 3, 1, 2, 4))
    return split_up.reshape(2 * frames, rows_here, columns, channels).astype(jnp.bfloat16)

def reference(latent_features, attn_gain, w_query, w_key, w_value, w_proj, unit_gain, conv_weight, upsample_weight):
    frames, rows_here, columns, channels = latent_features.shape
    score_scale = 1.0 / math.sqrt(channels)
    normed = rms_scale(latent_features, attn_gain).astype(jnp.bfloat16)
    flattened = normed.reshape(frames, rows_here * columns, channels)
    queries = jnp.dot(flattened, w_query, preferred_element_type=jnp.float32).astype(jnp.bfloat16)
    key_rows = jnp.dot(flattened, w_key, preferred_element_type=jnp.float32).astype(jnp.bfloat16)
    value_rows = jnp.dot(flattened, w_value, preferred_element_type=jnp.float32).astype(jnp.bfloat16)

    def one_frame(triple):
        query_block, key_block, value_block = triple
        scores = jnp.dot(query_block, key_block.T, preferred_element_type=jnp.float32) * score_scale
        row_max = lax.optimization_barrier(jnp.max(scores, axis=-1, keepdims=True))
        weights = jnp.exp(scores - row_max)
        weight_sum = lax.optimization_barrier(jnp.sum(weights, axis=-1, keepdims=True))
        numerator = jnp.dot(weights, value_block.astype(jnp.float32), precision=lax.Precision.HIGHEST)
        return (numerator / weight_sum).astype(jnp.bfloat16)
    attn_mixed = lax.map(one_frame, (queries, key_rows, value_rows))
    projected = jnp.dot(attn_mixed, w_proj, preferred_element_type=jnp.float32)
    attended = (latent_features.astype(jnp.float32) + projected.reshape(frames, rows_here, columns, channels)).astype(jnp.bfloat16)
    activated = jax.nn.silu(rms_scale(attended, unit_gain)).astype(jnp.bfloat16)
    conv_out = volume_conv(activated, conv_weight, ((2, 0), (1, 1), (1, 1)))
    unit_out = (attended.astype(jnp.float32) + conv_out).astype(jnp.bfloat16)
    padded = jnp.concatenate([jnp.zeros((2, rows_here, columns, channels), jnp.bfloat16), unit_out], axis=0)
    return alternate(time_conv(padded, upsample_weight))
```

```python
import math

import jax
import jax.numpy as jnp
from jax import lax
from jax.experimental import pallas as pl
from jax.experimental.pallas import tpu as pltpu
from jax.sharding import PartitionSpec as P

epsilon = 1e-06
MESH = pl.DeviceIdType.MESH
C = 384
W = 160
PART = 256
HALF = 128
PARTS = 8
BLOCK = 672
SCALE = math.log2(math.e) / math.sqrt(C)

PLACE = (0, 2, 3, 1)
STEPS = (
    ((
        ("zo", "part"), ("xo", "part"), ("xo", 1), ("zo", 1), ("X", "part", 0, 3, 0), ("X", "part", 0, 1, 0),
        ("X", "part", 0, 3, 1), ("X", "part", 0, 1, 1), ("X", 1, 0, 3, 0), ("X", 1, 0, 1, 0), ("Z", "part", 3, 0),
        ("Z", "part", 1, 1), ("X", 1, 0, 3, 1), ("X", 1, 0, 1, 1), ("X", "part", 0, 2, 0), ("X", "part", 0, 2, 1),
        ("YO", 0), ("Z", "part", 3, 1), ("Z", "part", 1, 0), ("xo", 0), ("X", 1, 0, 2, 0), ("X", "part", 3, 1, 0),
        ("X", "part", 3, 3, 0), ("X", "part", 1, 1, 1), ("X", "part", 1, 3, 1), ("X", "part", 3, 3, 1),
        ("X", 1, 0, 2, 1),
    ), (
        ("zo", "part"), ("xo", "part"), ("xo", 1), ("X", "part", 0, 3, 0), ("X", "part", 0, 1, 0),
        ("X", "part", 0, 3, 1), ("X", "part", 0, 1, 1), ("X", 1, 0, 3, 0), ("X", 1, 0, 1, 0), ("X", 1, 0, 3, 1),
        ("X", 1, 0, 1, 1), ("X", "part", 0, 2, 0), ("X", "part", 0, 2, 1), ("YO", 0), ("X", 1, 0, 2, 0),
        ("Z", "part", 3, 0), ("Z", "part", 1, 1), ("zo", 1), ("X", 1, 0, 2, 1),
    ), ("pr", 1, 0)),
    ((
        ("X", "part", 1, 3, 0), ("X", "part", 3, 1, 1), ("Y", 0, 3, 0), ("Y", 0, 1, 1), ("X", "part", 1, 1, 0),
        ("X", 0, 0, 3, 0), ("Z", 1, 3, 0), ("Z", 1, 1, 1), ("zo", 0), ("X", 0, 0, 1, 0), ("X", 0, 0, 3, 1),
        ("X", "part", 3, 2, 0), ("Y", 0, 3, 1), ("Y", 0, 1, 0), ("X", 0, 0, 1, 1), ("X", "part", 1, 2, 0),
        ("X", "part", 1, 2, 1), ("YO", 1), ("Z", 1, 3, 1), ("Z", 1, 1, 0), ("X", "part", 3, 2, 1), ("YO", 3),
        ("X", 0, 0, 2, 0), ("Z", "part", 2, 0), ("Z", "part", 2, 1), ("Y", 0, 2, 0), ("Y", 0, 2, 1), ("K", 0),
        ("X", 1, 3, 1, 0), ("X", 1, 3, 3, 0), ("X", 1, 1, 1, 1), ("X", 1, 1, 3, 1), ("X", 0, 0, 2, 1),
        ("Y", 1, 3, 0), ("Y", 1, 1, 1), ("X", 1, 3, 3, 1),
    ), (
        ("Z", "part", 3, 1), ("Z", "part", 1, 0), ("xo", 0), ("X", "part", 3, 3, 0), ("X", "part", 3, 1, 0),
        ("Y", 0, 3, 0), ("Y", 0, 1, 1), ("X", "part", 1, 3, 1), ("X", "part", 1, 1, 1), ("X", "part", 3, 1, 1),
        ("X", "part", 3, 3, 1), ("X", "part", 1, 1, 0), ("X", "part", 1, 3, 0), ("Y", 0, 3, 1), ("Y", 0, 1, 0),
        ("X", 0, 0, 1, 0), ("X", 0, 0, 3, 0), ("X", 0, 0, 1, 1), ("X", 0, 0, 3, 1), ("X", "part", 1, 2, 1),
        ("X", "part", 3, 2, 0), ("Y", 0, 2, 0), ("Y", 0, 2, 1), ("K", 0), ("X", "part", 3, 2, 1), ("YO", 3),
        ("X", "part", 1, 2, 0), ("YO", 1), ("Z", "part", 2, 0), ("Z", "part", 2, 1), ("X", 0, 0, 2, 0),
        ("X", 0, 0, 2, 1),
    ), ("un", 0)),
    ((
        ("X", 1, 3, 1, 1),
    ), (
        ("X", "part", 2, 3, 0), ("X", "part", 2, 1, 0), ("Z", 1, 3, 0), ("Z", 1, 1, 1), ("zo", 0),
        ("X", "part", 2, 3, 1), ("X", "part", 2, 1, 1), ("Y", 3, 3, 0), ("Y", 3, 1, 1),
    ), ("pr", 0, 0)),
    ((
        ("X", 1, 1, 3, 0), ("X", "part", 2, 3, 0), ("X", 1, 1, 1, 0), ("Y", 1, 3, 1), ("Y", 1, 1, 0),
        ("X", "part", 2, 3, 1), ("X", "part", 2, 1, 0), ("X", "part", 2, 1, 1), ("X", 1, 3, 2, 0), ("X", 1, 1, 2, 1),
        ("Y", 3, 3, 0), ("X", 1, 1, 2, 0), ("Y", 3, 1, 1), ("Z", 1, 2, 0), ("Z", 1, 2, 1), ("X", "part", 2, 2, 0),
        ("X", 1, 3, 2, 1),
    ), (
        ("Z", 1, 3, 1), ("Z", 1, 1, 0), ("X", "part", 2, 2, 0), ("X", 1, 3, 1, 0), ("Y", 3, 3, 1), ("Y", 3, 1, 0),
        ("X", 1, 3, 3, 0), ("X", 1, 1, 1, 1), ("X", 1, 1, 3, 1), ("X", "part", 2, 2, 1), ("YO", 2), ("Y", 1, 3, 0),
        ("Y", 1, 1, 1), ("X", 1, 3, 3, 1), ("X", 1, 3, 1, 1), ("X", 1, 1, 3, 0), ("X", 1, 1, 1, 0),
        ("X", 1, 3, 2, 0), ("Y", 1, 3, 1), ("Y", 1, 1, 0), ("X", 1, 1, 2, 1), ("X", 1, 3, 2, 1),
    ), ("pr", 1, 3)),
    ((
        ("X", "part", 2, 2, 1), ("YO", 2),
    ), (
        ("X", 1, 1, 2, 0),
    ), ("pr", 1, 1)),
    ((
        ("Y", 3, 3, 1), ("Y", 3, 1, 0),
    ), (
        ("Y", 3, 2, 0), ("Y", 3, 2, 1), ("K", 3),
    ), ("ask", 1)),
    ((
        ("Z", 0, 3, 0), ("Z", 0, 1, 1), ("X", 1, 2, 3, 0), ("X", 1, 2, 1, 0),
    ), (
        ("Z", 1, 2, 0), ("Z", 1, 2, 1),
    ), ("at", 1, 0)),
    ((
        ("X", 1, 2, 3, 1), ("X", 1, 2, 1, 1), ("Y", 1, 2, 0), ("Y", 1, 2, 1), ("K", 1), ("Z", 0, 3, 1),
        ("Z", 0, 1, 0),
    ), (
        ("Y", 2, 3, 0), ("Y", 2, 1, 1),
    ), ("at", 1, 1)),
    ((
        ("X", 0, 3, 3, 0), ("X", 0, 3, 1, 0), ("X", 0, 1, 3, 1), ("X", 0, 1, 1, 1), ("Y", 3, 2, 0), ("Y", 3, 2, 1),
        ("K", 3), ("X", 1, 2, 2, 0), ("X", 1, 2, 2, 1),
    ), (
        ("Z", 0, 3, 0), ("Z", 0, 1, 1), ("X", 1, 2, 3, 0), ("X", 1, 2, 1, 0), ("X", 1, 2, 3, 1), ("X", 1, 2, 1, 1),
        ("Y", 2, 3, 1), ("Y", 2, 1, 0), ("Z", 0, 3, 1), ("Z", 0, 1, 0), ("X", 0, 3, 3, 0), ("X", 0, 3, 1, 0),
        ("Y", 1, 2, 0), ("Y", 1, 2, 1), ("K", 1), ("X", 0, 1, 3, 1), ("X", 0, 1, 1, 1), ("X", 1, 2, 2, 0),
        ("X", 1, 2, 2, 1),
    ), ("pr", 1, 2)),
    ((
    ), (
        ("Y", 2, 2, 0), ("Y", 2, 2, 1), ("K", 2),
    ), ("at", 1, 2)),
    ((
        ("X", 0, 3, 3, 1), ("X", 0, 3, 1, 1), ("Y", 2, 3, 0), ("Y", 2, 1, 1), ("X", 0, 1, 3, 0), ("X", 0, 1, 1, 0),
    ), (
        ("Z", 0, 2, 0), ("X", 0, 3, 3, 1), ("X", 0, 3, 1, 1), ("Z", 0, 2, 1), ("X", 0, 1, 3, 0), ("X", 0, 1, 1, 0),
    ), ("fin", 1)),
    ((
        ("X", 0, 3, 2, 0), ("X", 0, 1, 2, 1),
    ), (
        ("X", 0, 3, 2, 0), ("X", 0, 1, 2, 1),
    ), ("un", 3)),
    ((
        ("Y", 2, 3, 1), ("Y", 2, 1, 0), ("X", 0, 3, 2, 1),
    ), (
        ("X", 0, 2, 3, 0), ("X", 0, 2, 1, 0), ("X", 0, 2, 3, 1), ("X", 0, 3, 2, 1),
    ), ("pr", 0, 3)),
    ((
        ("X", 0, 1, 2, 0),
    ), (
        ("X", 0, 1, 2, 0),
    ), ("pr", 0, 1)),
    ((
        ("Z", 0, 2, 0), ("Z", 0, 2, 1), ("Y", 2, 2, 0), ("Y", 2, 2, 1), ("K", 2),
    ), (
        ("X", 0, 2, 1, 1),
    ), ("ask", 0)),
    ((
    ), (
        ("X", 0, 2, 2, 0),
    ), ("at", 0, 0)),
    ((
    ), (
    ), ("at", 0, 1)),
    ((
        ("X", 0, 2, 3, 0), ("X", 0, 2, 1, 0), ("X", 0, 2, 3, 1), ("X", 0, 2, 1, 1), ("X", 0, 2, 2, 0),
        ("X", 0, 2, 2, 1),
    ), (
        ("X", 0, 2, 2, 1),
    ), ("pr", 0, 2)),
    ((
    ), (
    ), ("at", 0, 2)),
    ((
    ), (
    ), ("fin", 0)),
    ((
    ), (
    ), ("un", 1)),
    ((
    ), (
    ), ("un", 2)),
    ((
    ), (
    ), ("cv", 0)),
    ((
    ), (
    ), ("cv", 1)),
    ((
    ), (
    ), None),
)


def dot(left, right):
    return jnp.dot(left, right, preferred_element_type=jnp.float32)


def rms_scale(values, gain):
    widened = values.astype(jnp.float32)
    return widened * lax.rsqrt(jnp.mean(widened * widened, axis=-1, keepdims=True) + epsilon) * gain


def kernel(latent_hbm, shard_hbm, attn_gain_hbm, unit_gain_hbm, w_query_hbm, w_key_hbm, w_value_hbm, w_proj_hbm, upsample_hbm, out,
           latent, shard, attn_gain, unit_gain, cells, parts, packed, w_query, w_key_value, w_proj, upsample,
           keys, values, queries, numerator, row_max, attended, extended, conv_weight, sums, units,
           send_sems, grid_sems, y_sems, core_sems, frame_sems, local_sems):
    tm, rows = lax.axis_index("tm"), lax.axis_index("rows")
    z, x = rows // 4, lax.rem(rows, 4)
    core = lax.rem(tm, 2)
    z_lo = lax.rem(tm // 2, 4)
    y = tm // 8

    def ring(value, step):
        return lax.rem(value + (step % 4), 4)

    def to_z(step):
        return {"tm": tm, "rows": ring(z, step) * 4 + x}

    def to_x(step):
        return {"tm": tm, "rows": z * 4 + ring(x, step)}

    def to_y(step):
        return {"tm": (ring(y, step) * 4 + z_lo) * 2 + core, "rows": rows}

    sibling = {"tm": tm + 1 - 2 * core, "rows": rows}
    later = {"tm": lax.rem(tm + 1, 32), "rows": rows}
    before = {"tm": lax.rem(tm + 31, 32), "rows": rows}
    targets = {("z", 1): to_z(1), ("z", -1): to_z(-1), ("x", 1): to_x(1), ("x", -1): to_x(-1),
               ("y", 1): to_y(1), ("y", -1): to_y(-1), ("core", 1): sibling, ("tm", 1): later}

    barrier = pltpu.get_barrier_semaphore()
    greeted = list(targets.values()) + [before]
    for target in greeted:
        pl.semaphore_signal(barrier, inc=1, device_id=target, device_id_type=MESH)

    loads = []
    for source, target in ((shard_hbm, shard), (latent_hbm, latent), (attn_gain_hbm, attn_gain),
                           (unit_gain_hbm, unit_gain), (w_key_hbm, w_key_value.at[:, pl.ds(0, C)]), (w_value_hbm, w_key_value.at[:, pl.ds(C, C)]), (w_query_hbm, w_query),
                           (w_proj_hbm, w_proj), (upsample_hbm, upsample)):
        load = pltpu.make_async_copy(source, target, local_sems.at[2 + len(loads)])
        load.start()
        loads.append(load)
    loads[0].wait()

    for n in range(3):
        packed[pl.ds(BLOCK * n, 640)] = shard[:640, 128 * n:128 * n + 128]
        packed[pl.ds(BLOCK * n + 640, 32)] = jnp.concatenate(
            [shard[640:648, 128 * n:128 * n + 128].astype(jnp.float32), jnp.zeros((24, 128), jnp.float32)],
            axis=0).astype(jnp.bfloat16)
    packed[pl.ds(BLOCK * 3, 32)] = jnp.zeros((32, 128), jnp.bfloat16)

    pl.semaphore_wait(barrier, len(greeted))

    sent = {}

    def slot(dz, dx):
        return ring(z, dz) * 4 + ring(x, dx)

    def cell_unit(frame):
        return lambda dz, dx, h: cells.at[slot(dz, dx), pl.ds(W * frame + W // 2 * h, W // 2)]

    def part_unit(dz, dx, h):
        return parts.at[slot(dz, dx), pl.ds(PART * (core * 4 + y) + HALF * h, HALF)]

    def y_unit(dz, dy, h):
        return parts.at[pl.ds(4 * ring(z, dz), 4), pl.ds(PART * (core * 4 + ring(y, dy)) + HALF * h, HALF)]

    def push(tag, where, parts_of):
        index = sent.setdefault(tag, (len(sent), where, parts_of))[0]
        started(index, where, parts_of).start()

    def started(index, where, parts_of):
        source, target, recv_sem = parts_of()
        return pltpu.make_async_remote_copy(
            src_ref=source, dst_ref=target, send_sem=send_sems.at[index], recv_sem=recv_sem,
            device_id=targets[where], device_id_type=MESH)

    def arrive(region, recv_sem):
        pltpu.make_async_remote_copy(
            src_ref=region, dst_ref=region, send_sem=send_sems.at[0], recv_sem=recv_sem,
            device_id=sibling, device_id_type=MESH).wait_recv()

    grid_kinds = {"part": (part_unit, 0), 0: (cell_unit(0), 32), 1: (cell_unit(1), 64)}

    def grid_sem(kind, dz, dx, h):
        return grid_sems.at[grid_kinds[kind][1] + ((dz % 4) * 4 + dx % 4) * 2 + h]

    def grid_push(kind, dz, dx, h, axis, step, from_own=False):
        def parts_of():
            unit = grid_kinds[kind][0](dz, dx, h)
            sem = grid_sem(kind, dz - step, dx, h) if axis == "z" else grid_sem(kind, dz, dx - step, h)
            return own(kind, h) if from_own else unit, unit, sem

        push((kind, dz, dx, h, axis, step), (axis, step), parts_of)

    def grid_arrive(kind, dz, dx, h):
        arrive(grid_kinds[kind][0](dz, dx, h), grid_sem(kind, dz, dx, h))

    def y_sem(dz, dy, h):
        return y_sems.at[((dz % 4) * 4 + dy % 4) * 2 + h]

    def y_push(dz, dy, h, step):
        push(("y", dz, dy, h, step), ("y", step),
             lambda: (y_unit(dz, dy, h), y_unit(dz, dy, h), y_sem(dz, dy - step, h)))

    def y_arrive(dz, dy, h):
        arrive(y_unit(dz, dy, h), y_sem(dz, dy, h))

    def own(kind, h):
        if kind == "part":
            return packed.at[pl.ds(PART * (core * 4 + y) + HALF * h, HALF)]
        return latent.at[pl.ds(W * kind + W // 2 * h, W // 2)]

    ways = ((0, 1), (1, -1), (1, 1), (0, -1))
    forwarded = {(3, 0): 1, (1, 1): -1}

    def z_own(kind):
        for h, step in ways:
            grid_push(kind, 0, 0, h, "z", step, True)

    def x_out(kind, dz, h, from_own=False):
        first = 1 if h == 0 else -1
        grid_push(kind, dz, 0, h, "x", first, from_own)
        grid_push(kind, dz, 0, h, "x", -first, from_own)

    def x_own(kind):
        for h in range(2):
            x_out(kind, 0, h, True)

    def z_arrival(kind, dz, h):
        grid_arrive(kind, dz, 0, h)
        if (dz, h) in forwarded:
            grid_push(kind, dz, 0, h, "z", forwarded[dz, h])
        x_out(kind, dz, h)

    def x_arrival(kind, dz, dx, h):
        grid_arrive(kind, dz, dx, h)
        if (dx, h) in forwarded:
            grid_push(kind, dz, dx, h, "x", forwarded[dx, h])

    def y_own(dz):
        for h, step in ways:
            y_push(dz, 0, h, step)

    def y_arrival(dz, dy, h):
        y_arrive(dz, dy, h)
        if (dy, h) in forwarded:
            y_push(dz, dy, h, forwarded[dy, h])

    def core_unit(dz, which):
        return parts.at[pl.ds(4 * ring(z, dz), 4), pl.ds(PART * 4 * which, PART * 4)]

    def core_push(dz):
        push(("core", dz), ("core", 1), lambda: (core_unit(dz, core), core_unit(dz, core), core_sems.at[dz % 4]))

    def unpack(dz):
        arrive(core_unit(dz, 1 - core), core_sems.at[dz % 4])
        group = ring(z, dz)
        row = pl.multiple_of(96 * group, 32)

        def taps(loaded, first, count):
            for n in range(3):
                for i in range(3 * count):
                    target = pl.ds(pl.multiple_of(C * (first + i // 3) + row, 32), 96)
                    lanes = slice(C * (i % 3) + 128 * n, C * (i % 3) + 128 * n + 128)
                    conv_weight[target, lanes] = loaded[n][:, i].reshape(96, 128).astype(jnp.bfloat16)

        def load(n, start, count):
            block = parts[pl.ds(4 * group, 4), pl.ds(pl.multiple_of(BLOCK * n + start, 16), count)]
            return block.astype(jnp.float32).reshape(4, count // 24, 24, 128)

        def pair(j, carry):
            taps([load(n, 144 * j, 144) for n in range(3)], 2 * j, 2)
            return carry

        lax.fori_loop(0, 4, pair, 0)
        taps([load(n, 576, 96) for n in range(3)], 8, 1)

    def gained(ref):
        return ref[...].reshape(1, C)

    def project(frame, dz):
        if (frame, dz) == (1, 0):
            for load in loads[2:]:
                load.wait()
        group = ring(z, dz)

        def one(i, carry):
            block = cells[pl.ds(4 * group + 2 * i, 2), pl.ds(W * frame, W)].reshape(2 * W, C)
            normed = rms_scale(block, gained(attn_gain)).astype(jnp.bfloat16)
            place = pl.ds(pl.multiple_of(640 * PLACE[dz] + 2 * W * i, 64), 2 * W)
            both = dot(normed, w_key_value[...]).astype(jnp.bfloat16)
            keys[frame, place] = both[:, :C]
            values[frame, place, 0:C] = both[:, C:]
            return carry

        lax.fori_loop(0, 2, one, 0)

    def ask(frame):
        block = jnp.concatenate([cells[lax.rem(rows + 15 + b, 16), pl.ds(W * frame, W)] for b in range(3)], axis=0)
        normed = rms_scale(block, gained(attn_gain)).astype(jnp.bfloat16)
        queries[frame] = dot(normed, w_query[...]).astype(jnp.bfloat16)

    def attend(h, step):
        asked = (slice(0, 240), slice(240, 480), slice(0, 480))[step]
        place = slice(1920, 2560) if step == 2 else slice(0, 1920)
        scores = lax.dot_general(queries[h, asked], keys[h, place], (((1,), (1,)), ((), ())),
                                 preferred_element_type=jnp.float32)
        top = jnp.max(scores, axis=-1, keepdims=True)
        if step == 2:
            old = row_max[h][:, :1]
            top = jnp.maximum(top, old)
            rescale = jnp.exp2((old - top) * SCALE)
        weights = jnp.exp2((scores - top) * SCALE).astype(jnp.bfloat16)
        added = dot(weights, values[h, place])
        if step == 2:
            numerator[h] = numerator[h] * rescale + added
        else:
            numerator[h, asked] = added
            row_max[h, asked] = jnp.broadcast_to(top, (240, 128))

    def halo_unit(frame, b, half):
        return extended.at[pl.ds(W * frame + W // 2 * half, W // 2), pl.ds(C * b, C)]

    def finish(h):
        scale = 1.0 / numerator[h, :, C:]
        mixed = jnp.concatenate(
            [numerator[h, :, 128 * n:128 * n + 128] * scale for n in range(3)], axis=-1).astype(jnp.bfloat16)
        projected = dot(mixed, w_proj[...])
        for b in range(3):
            here = cells[lax.rem(rows + 15 + b, 16), pl.ds(W * h, W)].astype(jnp.float32)
            summed = (here + projected[W * b:W * b + W]).astype(jnp.bfloat16)
            if b == 1:
                attended[h] = summed
            scaled = rms_scale(summed, gained(unit_gain))
            activated = scaled / (1.0 + jnp.exp(-scaled))
            inside = jnp.logical_and(rows + b >= 1, rows + b <= 16)
            extended[pl.ds(W * (2 + h), W), C * b:C * b + C] = jnp.where(inside, activated, 0.0).astype(jnp.bfloat16)
            for half in range(2):
                push(("halo", h, b, half), ("tm", 1), lambda b=b, half=half: (
                    halo_unit(2 + h, b, half), halo_unit(h, b, half), frame_sems.at[6 * h + 2 * b + half]))

    def earlier(block):
        return jnp.where(tm > 0, block, jnp.zeros_like(block))

    def convolve(a, source, frames):
        block = extended[pl.ds(W * source, W * frames)]
        if source < 2:
            block = earlier(block)
        return dot(block, conv_weight[pl.ds(3 * C * a, 3 * C)])

    def halo(h):
        for b in range(3):
            for half in range(2):
                arrive(halo_unit(h, b, half), frame_sems.at[6 * h + 2 * b + half])

    def early_convolve(number):
        if number == 0:
            sums[pl.ds(W, W)] = convolve(2, 3, 1)
        else:
            halo(1)
            sums[pl.ds(0, W)] = convolve(1, 1, 1)
            sums[pl.ds(W, W)] += convolve(0, 1, 1)

    loads[1].wait()
    own_slice = pl.ds(pl.multiple_of(PART * (core * 4 + y), PART), PART)
    parts[rows, own_slice] = packed[own_slice]
    cells[rows] = latent[...]
    values[:, :, C:] = jnp.ones((2, 2560, 128), jnp.bfloat16)
    actions = {"zo": z_own, "xo": x_own, "Z": z_arrival, "X": x_arrival, "Y": y_arrival, "YO": y_own, "K": core_push,
               "pr": project, "ask": ask, "at": attend, "fin": finish, "un": unpack, "cv": early_convolve}

    def perform(operations):
        for name, *operands in operations:
            actions[name](*operands)

    for ahead, behind, work in STEPS:
        common = 0
        while common < min(len(ahead), len(behind)) and ahead[common] == behind[common]:
            common += 1
        perform(ahead[:common])
        if len(ahead) > common:
            pl.when(z_lo >= 2)(lambda: perform(ahead[common:]))
        if len(behind) > common:
            pl.when(z_lo < 2)(lambda: perform(behind[common:]))
        if work is not None:
            perform((work,))

    column = lax.broadcasted_iota(jnp.int32, (W, C), 0)

    def unit_half(frame, half):
        return units.at[pl.ds(W * frame + W // 2 * half, W // 2)]

    def unit(h, total):
        left = pltpu.roll(total[:, :C], 1, 0)
        right = pltpu.roll(total[:, 2 * C:], W - 1, 0)
        convolved = total[:, C:2 * C] + jnp.where(column > 0, left, 0.0) + jnp.where(column < W - 1, right, 0.0)
        units[pl.ds(W * (2 + h), W)] = (attended[h].astype(jnp.float32) + convolved).astype(jnp.bfloat16)
        for half in range(2):
            push(("unit", h, half), ("tm", 1), lambda half=half: (
                unit_half(2 + h, half), unit_half(h, half), frame_sems.at[12 + 2 * h + half]))

    def earlier_unit(h):
        for half in range(2):
            arrive(unit_half(h, half), frame_sems.at[12 + 2 * h + half])
        return earlier(units[pl.ds(W * h, W)])

    def put(h, stretched):
        out[2 * h] = stretched[:, :C]
        out[2 * h + 1] = stretched[:, C:]

    unit(1, sums[pl.ds(W, W)] + convolve(1, 2, 1))
    sums[pl.ds(0, W)] += convolve(2, 2, 1)
    last = dot(units[pl.ds(W * 3, W)], upsample[2])
    halo(0)
    unit(0, sums[pl.ds(0, W)] + convolve(0, 0, 1))
    newest = units[pl.ds(W * 2, W)]
    last = last + dot(newest, upsample[1])
    first = dot(newest, upsample[2])
    newest = earlier_unit(1)
    put(1, last + dot(newest, upsample[0]))
    first = first + dot(newest, upsample[1])
    put(0, first + dot(earlier_unit(0), upsample[0]))
    for entry in sent.values():
        started(*entry).wait_send()


def body(latent_features, attn_gain, w_query, w_key, w_value, w_proj, unit_gain, conv_weight, upsample_weight):
    vmem = pl.BlockSpec(memory_space=pltpu.VMEM)
    hbm = pl.BlockSpec(memory_space=pltpu.HBM)
    bf16, f32 = jnp.bfloat16, jnp.float32
    out = pl.pallas_call(
        kernel,
        out_shape=jax.ShapeDtypeStruct((4, W, C), f32),
        in_specs=[hbm] * 9,
        out_specs=vmem,
        scratch_shapes=[
            pltpu.VMEM((2 * W, C), bf16),
            pltpu.VMEM((648, C), bf16),
            pltpu.VMEM((C,), f32),
            pltpu.VMEM((C,), f32),
            pltpu.VMEM((16, 2 * W, C), bf16),
            pltpu.VMEM((16, PART * PARTS, 128), bf16),
            pltpu.VMEM((PART * PARTS, 128), bf16),
            pltpu.VMEM((C, C), bf16),
            pltpu.VMEM((C, 2 * C), bf16),
            pltpu.VMEM((C, C), bf16),
            pltpu.VMEM((3, C, 2 * C), bf16),
            pltpu.VMEM((2, 2560, C), bf16),
            pltpu.VMEM((2, 2560, C + 128), bf16),
            pltpu.VMEM((2, 3 * W, C), bf16),
            pltpu.VMEM((2, 3 * W, C + 128), f32),
            pltpu.VMEM((2, 3 * W, 128), f32),
            pltpu.VMEM((2, W, C), bf16),
            pltpu.VMEM((4 * W, 3 * C), bf16),
            pltpu.VMEM((9 * C, 3 * C), bf16),
            pltpu.VMEM((2 * W, 3 * C), f32),
            pltpu.VMEM((4 * W, C), bf16),
            pltpu.SemaphoreType.DMA((136,)),
            pltpu.SemaphoreType.DMA((96,)),
            pltpu.SemaphoreType.DMA((32,)),
            pltpu.SemaphoreType.DMA((4,)),
            pltpu.SemaphoreType.DMA((16,)),
            pltpu.SemaphoreType.DMA((11,)),
        ],
        compiler_params=pltpu.CompilerParams(
            collective_id=0, has_side_effects=True, vmem_limit_bytes=60 * 1024 * 1024),
    )(latent_features.reshape(2 * W, C), conv_weight.reshape(648, C), attn_gain, unit_gain,
      w_query, w_key, w_value, w_proj, upsample_weight)
    return out.astype(bf16).reshape(4, 1, W, C)


def solution(mesh):
    in_specs = (P("tm", "rows", None, None), P(), P(), P(), P(), P(), P(), P(None, None, None, "rows", None), P())
    return jax.shard_map(body, mesh=mesh, in_specs=in_specs, out_specs=P("tm", "rows", None, None), check_vma=False)
```

```python
import math

import jax
import jax.numpy as jnp
from jax import lax
from jax.experimental import pallas as pl
from jax.experimental.pallas import tpu as pltpu
from jax.sharding import PartitionSpec as P

epsilon = 1e-06
MESH = pl.DeviceIdType.MESH
C = 384
W = 160
PART = 256
HALF = 128
PARTS = 8
BLOCK = 672
SCALE = math.log2(math.e) / math.sqrt(C)

PLACE = (0, 2, 3, 1)
STEPS = (
    ((
        ("zo", "part"), ("xo", "part"), ("xo", 1), ("zo", 1), ("X", "part", 0, 3, 0), ("X", "part", 0, 1, 0),
        ("X", "part", 0, 3, 1), ("X", "part", 0, 1, 1), ("X", 1, 0, 3, 0), ("X", 1, 0, 1, 0), ("Z", "part", 3, 0),
        ("Z", "part", 1, 1), ("X", 1, 0, 3, 1), ("X", 1, 0, 1, 1), ("X", "part", 0, 2, 0), ("X", "part", 0, 2, 1),
        ("YO", 0), ("Z", "part", 3, 1), ("Z", "part", 1, 0), ("xo", 0), ("X", 1, 0, 2, 0), ("X", "part", 3, 1, 0),
        ("X", "part", 3, 3, 0), ("X", "part", 1, 1, 1), ("X", "part", 1, 3, 1), ("X", "part", 3, 3, 1),
        ("X", 1, 0, 2, 1),
    ), (
        ("zo", "part"), ("xo", "part"), ("xo", 1), ("X", "part", 0, 3, 0), ("X", "part", 0, 1, 0),
        ("X", "part", 0, 3, 1), ("X", "part", 0, 1, 1), ("X", 1, 0, 3, 0), ("X", 1, 0, 1, 0), ("X", 1, 0, 3, 1),
        ("X", 1, 0, 1, 1), ("X", "part", 0, 2, 0), ("X", "part", 0, 2, 1), ("YO", 0), ("X", 1, 0, 2, 0),
        ("Z", "part", 3, 0), ("Z", "part", 1, 1), ("zo", 1), ("X", 1, 0, 2, 1),
    ), ("pr", 1, 0)),
    ((
        ("X", "part", 1, 3, 0), ("X", "part", 3, 1, 1), ("Y", 0, 3, 0), ("Y", 0, 1, 1), ("X", "part", 1, 1, 0),
        ("X", 0, 0, 3, 0), ("Z", 1, 3, 0), ("Z", 1, 1, 1), ("zo", 0), ("X", 0, 0, 1, 0), ("X", 0, 0, 3, 1),
        ("X", "part", 3, 2, 0), ("Y", 0, 3, 1), ("Y", 0, 1, 0), ("X", 0, 0, 1, 1), ("X", "part", 1, 2, 0),
        ("X", "part", 1, 2, 1), ("YO", 1), ("Z", 1, 3, 1), ("Z", 1, 1, 0), ("X", "part", 3, 2, 1), ("YO", 3),
        ("X", 0, 0, 2, 0), ("Z", "part", 2, 0), ("Z", "part", 2, 1), ("Y", 0, 2, 0), ("Y", 0, 2, 1),
        ("X", 1, 3, 1, 0), ("X", 1, 3, 3, 0), ("X", 1, 1, 1, 1), ("X", 1, 1, 3, 1), ("X", 0, 0, 2, 1),
        ("Y", 1, 3, 0), ("Y", 1, 1, 1), ("X", 1, 3, 3, 1), ("X", 1, 3, 1, 1), ("X", 1, 1, 3, 0),
        ("X", "part", 2, 3, 0), ("X", 1, 1, 1, 0), ("Y", 1, 3, 1), ("Y", 1, 1, 0), ("X", "part", 2, 3, 1),
        ("X", "part", 2, 1, 0), ("X", "part", 2, 1, 1), ("X", 1, 3, 2, 0), ("X", 1, 1, 2, 1), ("Y", 3, 3, 0),
        ("X", 1, 1, 2, 0), ("Y", 3, 1, 1),
    ), (
        ("Z", "part", 3, 1), ("Z", "part", 1, 0), ("xo", 0), ("X", "part", 3, 3, 0), ("X", "part", 3, 1, 0),
        ("Y", 0, 3, 0), ("Y", 0, 1, 1), ("X", "part", 1, 3, 1), ("X", "part", 1, 1, 1), ("X", "part", 3, 1, 1),
        ("X", "part", 3, 3, 1), ("X", "part", 1, 1, 0), ("X", "part", 1, 3, 0), ("Y", 0, 3, 1), ("Y", 0, 1, 0),
        ("X", 0, 0, 1, 0), ("X", 0, 0, 3, 0), ("X", 0, 0, 1, 1), ("X", 0, 0, 3, 1), ("X", "part", 1, 2, 1),
        ("X", "part", 3, 2, 0), ("Y", 0, 2, 0), ("Y", 0, 2, 1), ("X", "part", 3, 2, 1), ("YO", 3),
        ("X", "part", 1, 2, 0), ("YO", 1), ("Z", "part", 2, 0), ("Z", "part", 2, 1), ("X", 0, 0, 2, 0),
        ("X", 0, 0, 2, 1), ("X", "part", 2, 3, 0), ("Z", 1, 3, 0), ("X", "part", 2, 1, 0), ("Z", 1, 1, 1), ("zo", 0),
        ("X", "part", 2, 3, 1), ("X", "part", 2, 1, 1),
    ), ("un", 0)),
    ((
        ("Z", 1, 2, 0), ("Z", 1, 2, 1), ("X", "part", 2, 2, 0), ("X", 1, 3, 2, 1),
    ), (
        ("Y", 3, 3, 0), ("Y", 3, 1, 1),
    ), ("pr", 0, 0)),
    ((
        ("X", "part", 2, 2, 1), ("YO", 2), ("Y", 3, 3, 1), ("Y", 3, 1, 0),
    ), (
        ("X", "part", 2, 2, 0), ("Z", 1, 3, 1), ("Z", 1, 1, 0), ("X", 1, 3, 1, 0), ("X", 1, 3, 3, 0), ("Y", 3, 3, 1),
        ("Y", 3, 1, 0), ("X", 1, 1, 1, 1), ("X", 1, 1, 3, 1), ("X", "part", 2, 2, 1), ("YO", 2), ("X", 1, 3, 3, 1),
        ("X", 1, 3, 1, 1), ("Y", 1, 3, 0), ("Y", 1, 1, 1), ("X", 1, 1, 3, 0), ("X", 1, 1, 1, 0), ("X", 1, 3, 2, 0),
        ("X", 1, 1, 2, 1), ("Y", 1, 3, 1), ("Y", 1, 1, 0), ("X", 1, 3, 2, 1),
    ), ("pr", 1, 3)),
    ((
        ("Z", 0, 3, 0), ("Z", 0, 1, 1),
    ), (
        ("X", 1, 1, 2, 0),
    ), ("pr", 1, 1)),
    ((
        ("X", 1, 2, 3, 0), ("X", 1, 2, 1, 0),
    ), (
    ), ("ask", 1)),
    ((
        ("Y", 1, 2, 0), ("Y", 1, 2, 1), ("Z", 0, 3, 1), ("X", 1, 2, 3, 1), ("Z", 0, 1, 0), ("X", 1, 2, 1, 1),
    ), (
        ("Y", 3, 2, 0), ("Y", 3, 2, 1),
    ), ("at", 1, 0)),
    ((
        ("X", 0, 3, 3, 0), ("X", 0, 3, 1, 0),
    ), (
        ("Z", 1, 2, 0), ("Z", 1, 2, 1),
    ), ("at", 1, 1)),
    ((
        ("X", 0, 1, 3, 1), ("Y", 3, 2, 0), ("X", 0, 1, 1, 1), ("Y", 3, 2, 1), ("X", 1, 2, 2, 0), ("X", 0, 3, 1, 1),
        ("X", 0, 3, 3, 1), ("X", 0, 1, 1, 0), ("Y", 2, 3, 0), ("Y", 2, 1, 1), ("X", 0, 1, 3, 0), ("X", 1, 2, 2, 1),
    ), (
        ("Y", 2, 3, 0), ("Y", 2, 1, 1), ("Z", 0, 3, 0), ("Z", 0, 1, 1), ("X", 1, 2, 3, 0), ("X", 1, 2, 1, 0),
        ("Y", 2, 3, 1), ("Y", 2, 1, 0), ("Z", 0, 3, 1), ("Z", 0, 1, 0), ("X", 1, 2, 3, 1), ("X", 1, 2, 1, 1),
        ("X", 0, 3, 3, 0), ("X", 0, 3, 1, 0), ("Y", 1, 2, 0), ("Y", 1, 2, 1), ("X", 0, 1, 3, 1), ("X", 0, 1, 1, 1),
        ("X", 1, 2, 2, 0), ("X", 0, 3, 1, 1), ("Y", 2, 2, 0), ("Z", 0, 2, 0), ("Y", 2, 2, 1), ("Z", 0, 2, 1),
        ("X", 0, 3, 3, 1), ("X", 0, 1, 1, 0), ("X", 0, 1, 3, 0), ("X", 1, 2, 2, 1),
    ), ("pr", 1, 2)),
    ((
    ), (
    ), ("at", 1, 2)),
    ((
        ("X", 0, 3, 2, 0), ("X", 0, 1, 2, 1), ("Y", 2, 3, 1), ("Y", 2, 1, 0), ("X", 0, 3, 2, 1),
    ), (
        ("X", 0, 3, 2, 0), ("X", 0, 1, 2, 1),
    ), ("fin", 1)),
    ((
        ("X", 0, 1, 2, 0), ("Z", 0, 2, 0), ("Z", 0, 2, 1), ("Y", 2, 2, 0), ("Y", 2, 2, 1),
    ), (
        ("X", 0, 2, 3, 0), ("X", 0, 3, 2, 1), ("X", 0, 2, 3, 1), ("X", 0, 2, 1, 0),
    ), ("un", 3)),
    ((
    ), (
        ("X", 0, 1, 2, 0), ("X", 0, 2, 1, 1),
    ), ("pr", 0, 3)),
    ((
    ), (
    ), ("pr", 0, 1)),
    ((
        ("X", 0, 2, 3, 0), ("X", 0, 2, 1, 0),
    ), (
    ), ("ask", 0)),
    ((
        ("X", 0, 2, 3, 1), ("X", 0, 2, 1, 1),
    ), (
        ("X", 0, 2, 2, 0),
    ), ("at", 0, 0)),
    ((
    ), (
        ("X", 0, 2, 2, 1),
    ), ("un", 1)),
    ((
        ("X", 0, 2, 2, 0),
    ), (
    ), ("at", 0, 1)),
    ((
        ("X", 0, 2, 2, 1),
    ), (
    ), ("un", 2)),
    ((
    ), (
    ), ("pr", 0, 2)),
    ((
    ), (
    ), ("at", 0, 2)),
    ((
    ), (
    ), ("fin", 0)),
    ((
    ), (
    ), None),
)


def dot(left, right):
    return jnp.dot(left, right, preferred_element_type=jnp.float32)


def rms_scale(values, gain):
    widened = values.astype(jnp.float32)
    return widened * lax.rsqrt(jnp.mean(widened * widened, axis=-1, keepdims=True) + epsilon) * gain


def kernel(latent_hbm, shard_hbm, attn_gain_hbm, unit_gain_hbm, w_query_hbm, w_key_hbm, w_value_hbm, w_proj_hbm, upsample_hbm, out,
           latent, shard, attn_gain, unit_gain, cells, parts, packed, w_query, w_key_value, w_proj, upsample,
           keys, values, queries, numerator, row_max, attended, extended, conv_weight, sums, units, carried,
           send_sems, grid_sems, y_sems, core_sems, frame_sems, local_sems):
    tm, rows = lax.axis_index("tm"), lax.axis_index("rows")
    z, x = rows // 4, lax.rem(rows, 4)
    core = lax.rem(tm, 2)
    z_lo = lax.rem(tm // 2, 4)
    y = tm // 8

    def ring(value, step):
        return lax.rem(value + (step % 4), 4)

    def to_z(step):
        return {"tm": tm, "rows": ring(z, step) * 4 + x}

    def to_x(step):
        return {"tm": tm, "rows": z * 4 + ring(x, step)}

    def to_y(step):
        return {"tm": (ring(y, step) * 4 + z_lo) * 2 + core, "rows": rows}

    sibling = {"tm": tm + 1 - 2 * core, "rows": rows}
    later = {"tm": lax.rem(tm + 1, 32), "rows": rows}
    before = {"tm": lax.rem(tm + 31, 32), "rows": rows}
    targets = {("z", 1): to_z(1), ("z", -1): to_z(-1), ("x", 1): to_x(1), ("x", -1): to_x(-1),
               ("y", 1): to_y(1), ("y", -1): to_y(-1), ("core", 1): sibling, ("tm", 1): later}

    barrier = pltpu.get_barrier_semaphore()
    greeted = list(targets.values()) + [before]
    for target in greeted:
        pl.semaphore_signal(barrier, inc=1, device_id=target, device_id_type=MESH)

    loads = []
    for source, target in ((shard_hbm, shard), (latent_hbm, latent), (attn_gain_hbm, attn_gain),
                           (unit_gain_hbm, unit_gain), (w_key_hbm, w_key_value.at[:, pl.ds(0, C)]), (w_value_hbm, w_key_value.at[:, pl.ds(C, C)]), (w_query_hbm, w_query),
                           (w_proj_hbm, w_proj), (upsample_hbm, upsample)):
        load = pltpu.make_async_copy(source, target, local_sems.at[2 + len(loads)])
        load.start()
        loads.append(load)
    loads[0].wait()

    for n in range(3):
        packed[pl.ds(BLOCK * n, 640)] = shard[:640, 128 * n:128 * n + 128]
        packed[pl.ds(BLOCK * n + 640, 32)] = jnp.concatenate(
            [shard[640:648, 128 * n:128 * n + 128].astype(jnp.float32), jnp.zeros((24, 128), jnp.float32)],
            axis=0).astype(jnp.bfloat16)
    packed[pl.ds(BLOCK * 3, 32)] = jnp.zeros((32, 128), jnp.bfloat16)

    pl.semaphore_wait(barrier, len(greeted))

    sent = {}

    def slot(dz, dx):
        return ring(z, dz) * 4 + ring(x, dx)

    def cell_unit(frame):
        return lambda dz, dx, h: cells.at[slot(dz, dx), pl.ds(W * frame + W // 2 * h, W // 2)]

    def part_unit(dz, dx, h):
        return parts.at[slot(dz, dx), pl.ds(PART * (core * 4 + y) + HALF * h, HALF)]

    def y_unit(dz, dy, h):
        return parts.at[pl.ds(4 * ring(z, dz), 4), pl.ds(PART * (core * 4 + ring(y, dy)) + HALF * h, HALF)]

    def push(tag, where, parts_of):
        index = sent.setdefault(tag, (len(sent), where, parts_of))[0]
        started(index, where, parts_of).start()

    def started(index, where, parts_of):
        source, target, recv_sem = parts_of()
        return pltpu.make_async_remote_copy(
            src_ref=source, dst_ref=target, send_sem=send_sems.at[index], recv_sem=recv_sem,
            device_id=targets[where], device_id_type=MESH)

    def arrive(region, recv_sem):
        pltpu.make_async_remote_copy(
            src_ref=region, dst_ref=region, send_sem=send_sems.at[0], recv_sem=recv_sem,
            device_id=sibling, device_id_type=MESH).wait_recv()

    grid_kinds = {"part": (part_unit, 0), 0: (cell_unit(0), 32), 1: (cell_unit(1), 64)}

    def grid_sem(kind, dz, dx, h):
        return grid_sems.at[grid_kinds[kind][1] + ((dz % 4) * 4 + dx % 4) * 2 + h]

    def grid_push(kind, dz, dx, h, axis, step, from_own=False):
        def parts_of():
            unit = grid_kinds[kind][0](dz, dx, h)
            sem = grid_sem(kind, dz - step, dx, h) if axis == "z" else grid_sem(kind, dz, dx - step, h)
            return own(kind, h) if from_own else unit, unit, sem

        push((kind, dz, dx, h, axis, step), (axis, step), parts_of)

    def grid_arrive(kind, dz, dx, h):
        arrive(grid_kinds[kind][0](dz, dx, h), grid_sem(kind, dz, dx, h))

    def y_sem(dz, dy, h):
        return y_sems.at[((dz % 4) * 4 + dy % 4) * 2 + h]

    def y_push(dz, dy, h, step):
        push(("y", dz, dy, h, step), ("y", step),
             lambda: (y_unit(dz, dy, h), y_unit(dz, dy, h), y_sem(dz, dy - step, h)))

    def y_arrive(dz, dy, h):
        arrive(y_unit(dz, dy, h), y_sem(dz, dy, h))

    def own(kind, h):
        if kind == "part":
            return packed.at[pl.ds(PART * (core * 4 + y) + HALF * h, HALF)]
        return latent.at[pl.ds(W * kind + W // 2 * h, W // 2)]

    ways = ((0, 1), (1, -1), (1, 1), (0, -1))
    forwarded = {(3, 0): 1, (1, 1): -1}

    def z_own(kind):
        for h, step in ways:
            grid_push(kind, 0, 0, h, "z", step, True)

    def x_out(kind, dz, h, from_own=False):
        first = 1 if h == 0 else -1
        grid_push(kind, dz, 0, h, "x", first, from_own)
        grid_push(kind, dz, 0, h, "x", -first, from_own)

    def x_own(kind):
        for h in range(2):
            x_out(kind, 0, h, True)

    def z_arrival(kind, dz, h):
        grid_arrive(kind, dz, 0, h)
        if (dz, h) in forwarded:
            grid_push(kind, dz, 0, h, "z", forwarded[dz, h])
        x_out(kind, dz, h)

    def x_arrival(kind, dz, dx, h):
        grid_arrive(kind, dz, dx, h)
        if (dx, h) in forwarded:
            grid_push(kind, dz, dx, h, "x", forwarded[dx, h])

    def y_own(dz):
        for h, step in ways:
            y_push(dz, 0, h, step)
        for h in range(2):
            core_push(dz, 0, h)

    def y_arrival(dz, dy, h):
        y_arrive(dz, dy, h)
        if (dy, h) in forwarded:
            y_push(dz, dy, h, forwarded[dy, h])
        core_push(dz, dy, h)

    def core_unit(dz, dy, h, which):
        return parts.at[pl.ds(4 * ring(z, dz), 4), pl.ds(PART * (which * 4 + ring(y, dy)) + HALF * h, HALF)]

    def core_sem(dz, dy, h):
        return core_sems.at[((dz % 4) * 4 + dy % 4) * 2 + h]

    def core_push(dz, dy, h):
        push(("core", dz, dy, h), ("core", 1),
             lambda: (core_unit(dz, dy, h, core), core_unit(dz, dy, h, core), core_sem(dz, dy, h)))

    def unpack(dz):
        for dy in range(4):
            for h in range(2):
                arrive(core_unit(dz, dy, h, 1 - core), core_sem(dz, dy, h))
        group = ring(z, dz)
        row = pl.multiple_of(96 * group, 32)

        def taps(loaded, first, count):
            for n in range(3):
                for i in range(3 * count):
                    target = pl.ds(pl.multiple_of(C * (first + i // 3) + row, 32), 96)
                    lanes = slice(C * (i % 3) + 128 * n, C * (i % 3) + 128 * n + 128)
                    conv_weight[target, lanes] = loaded[n][:, i].reshape(96, 128).astype(jnp.bfloat16)

        def load(n, start, count):
            block = parts[pl.ds(4 * group, 4), pl.ds(pl.multiple_of(BLOCK * n + start, 16), count)]
            return block.astype(jnp.float32).reshape(4, count // 24, 24, 128)

        def pair(j, carry):
            taps([load(n, 144 * j, 144) for n in range(3)], 2 * j, 2)
            return carry

        lax.fori_loop(0, 4, pair, 0)
        taps([load(n, 576, 96) for n in range(3)], 8, 1)

    def gained(ref):
        return ref[...].reshape(1, C)

    def project(frame, dz):
        if (frame, dz) == (1, 0):
            for load in loads[2:]:
                load.wait()
        group = ring(z, dz)

        def one(i, carry):
            block = cells[pl.ds(4 * group + 2 * i, 2), pl.ds(W * frame, W)].reshape(2 * W, C)
            normed = rms_scale(block, gained(attn_gain)).astype(jnp.bfloat16)
            place = pl.ds(pl.multiple_of(640 * PLACE[dz] + 2 * W * i, 64), 2 * W)
            both = dot(normed, w_key_value[...]).astype(jnp.bfloat16)
            keys[frame, place] = both[:, :C]
            values[frame, place, 0:C] = both[:, C:]
            return carry

        lax.fori_loop(0, 2, one, 0)

    def ask(frame):
        block = jnp.concatenate([cells[lax.rem(rows + 15 + b, 16), pl.ds(W * frame, W)] for b in range(3)], axis=0)
        normed = rms_scale(block, gained(attn_gain)).astype(jnp.bfloat16)
        queries[frame] = dot(normed, w_query[...]).astype(jnp.bfloat16)

    def attend(h, step):
        asked = (slice(0, 240), slice(240, 480), slice(0, 480))[step]
        place = slice(1920, 2560) if step == 2 else slice(0, 1920)
        scores = lax.dot_general(queries[h, asked], keys[h, place], (((1,), (1,)), ((), ())),
                                 preferred_element_type=jnp.float32)
        top = jnp.max(scores, axis=-1, keepdims=True)
        if step == 2:
            old = row_max[h][:, :1]
            top = jnp.maximum(top, old)
            rescale = jnp.exp2((old - top) * SCALE)
        weights = jnp.exp2((scores - top) * SCALE).astype(jnp.bfloat16)
        added = dot(weights, values[h, place])
        if step == 2:
            numerator[h] = numerator[h] * rescale + added
        else:
            numerator[h, asked] = added
            row_max[h, asked] = jnp.broadcast_to(top, (240, 128))

    def halo_unit(frame, b, half):
        return extended.at[pl.ds(W * frame + W // 2 * half, W // 2), pl.ds(C * b, C)]

    def finish(h):
        scale = 1.0 / numerator[h, :, C:]
        mixed = jnp.concatenate(
            [numerator[h, :, 128 * n:128 * n + 128] * scale for n in range(3)], axis=-1).astype(jnp.bfloat16)
        projected = dot(mixed, w_proj[...])
        for b in range(3):
            here = cells[lax.rem(rows + 15 + b, 16), pl.ds(W * h, W)].astype(jnp.float32)
            summed = (here + projected[W * b:W * b + W]).astype(jnp.bfloat16)
            if b == 1:
                attended[h] = summed
            scaled = rms_scale(summed, gained(unit_gain))
            activated = scaled / (1.0 + jnp.exp(-scaled))
            inside = jnp.logical_and(rows + b >= 1, rows + b <= 16)
            extended[pl.ds(W * (2 + h), W), C * b:C * b + C] = jnp.where(inside, activated, 0.0).astype(jnp.bfloat16)
            for half in range(2 * h):
                push(("halo", h, b, half), ("tm", 1), lambda b=b, half=half: (
                    halo_unit(2 + h, b, half), halo_unit(h, b, half), frame_sems.at[6 * h + 2 * b + half]))

    def earlier(block):
        return jnp.where(tm > 0, block, jnp.zeros_like(block))

    def convolve(a, source, frames):
        block = extended[pl.ds(W * source, W * frames)]
        if source < 2:
            block = earlier(block)
        return dot(block, conv_weight[pl.ds(3 * C * a, 3 * C)])

    def halo():
        for b in range(3):
            for half in range(2):
                arrive(halo_unit(1, b, half), frame_sems.at[6 + 2 * b + half])

    column = lax.broadcasted_iota(jnp.int32, (W, C), 0)

    def joined(total):
        left = pltpu.roll(total[:, :C], 1, 0)
        right = pltpu.roll(total[:, 2 * C:], W - 1, 0)
        return total[:, C:2 * C] + jnp.where(column > 0, left, 0.0) + jnp.where(column < W - 1, right, 0.0)

    def carried_half(place, half):
        return carried.at[pl.ds(W * place + W // 2 * half, W // 2)]

    loads[1].wait()
    own_slice = pl.ds(pl.multiple_of(PART * (core * 4 + y), PART), PART)
    parts[rows, own_slice] = packed[own_slice]
    cells[rows] = latent[...]
    values[:, :, C:] = jnp.ones((2, 2560, 128), jnp.bfloat16)
    actions = {"zo": z_own, "xo": x_own, "Z": z_arrival, "X": x_arrival, "Y": y_arrival, "YO": y_own,
               "pr": project, "ask": ask, "at": attend, "fin": finish, "un": unpack}

    def perform(operations):
        for name, *operands in operations:
            actions[name](*operands)

    for ahead, behind, work in STEPS:
        common = 0
        while common < min(len(ahead), len(behind)) and ahead[common] == behind[common]:
            common += 1
        perform(ahead[:common])
        if len(ahead) > common:
            pl.when(z_lo >= 2)(lambda: perform(ahead[common:]))
        if len(behind) > common:
            pl.when(z_lo < 2)(lambda: perform(behind[common:]))
        if work is not None:
            perform((work,))

    carried[pl.ds(W, W)] = joined(convolve(0, 2, 1)).astype(jnp.bfloat16)
    for half in range(2):
        push(("carried", half), ("tm", 1), lambda half=half: (
            carried_half(1, half), carried_half(0, half), frame_sems.at[half]))

    def unit_half(frame, half):
        return units.at[pl.ds(W * frame + W // 2 * half, W // 2)]

    def unit(h, convolved):
        units[pl.ds(W * (2 + h), W)] = (attended[h].astype(jnp.float32) + convolved).astype(jnp.bfloat16)
        for half in range(2):
            push(("unit", h, half), ("tm", 1), lambda half=half: (
                unit_half(2 + h, half), unit_half(h, half), frame_sems.at[12 + 2 * h + half]))

    def earlier_unit(h):
        for half in range(2):
            arrive(unit_half(h, half), frame_sems.at[12 + 2 * h + half])
        return earlier(units[pl.ds(W * h, W)])

    def put(h, stretched):
        out[2 * h] = stretched[:, :C]
        out[2 * h + 1] = stretched[:, C:]

    sums[...] = convolve(2, 2, 2)
    sums[pl.ds(W, W)] += convolve(1, 2, 1)
    halo()
    unit(1, joined(sums[pl.ds(W, W)] + convolve(0, 1, 1)))
    convolved = joined(sums[pl.ds(0, W)] + convolve(1, 1, 1))
    last = dot(units[pl.ds(W * 3, W)], upsample[2])
    for half in range(2):
        arrive(carried_half(0, half), frame_sems.at[half])
    unit(0, convolved + earlier(carried[pl.ds(0, W)]).astype(jnp.float32))
    newest = units[pl.ds(W * 2, W)]
    last = last + dot(newest, upsample[1])
    first = dot(newest, upsample[2])
    newest = earlier_unit(1)
    put(1, last + dot(newest, upsample[0]))
    first = first + dot(newest, upsample[1])
    put(0, first + dot(earlier_unit(0), upsample[0]))
    for entry in sent.values():
        started(*entry).wait_send()


def body(latent_features, attn_gain, w_query, w_key, w_value, w_proj, unit_gain, conv_weight, upsample_weight):
    vmem = pl.BlockSpec(memory_space=pltpu.VMEM)
    hbm = pl.BlockSpec(memory_space=pltpu.HBM)
    bf16, f32 = jnp.bfloat16, jnp.float32
    out = pl.pallas_call(
        kernel,
        out_shape=jax.ShapeDtypeStruct((4, W, C), f32),
        in_specs=[hbm] * 9,
        out_specs=vmem,
        scratch_shapes=[
            pltpu.VMEM((2 * W, C), bf16),
            pltpu.VMEM((648, C), bf16),
            pltpu.VMEM((C,), f32),
            pltpu.VMEM((C,), f32),
            pltpu.VMEM((16, 2 * W, C), bf16),
            pltpu.VMEM((16, PART * PARTS, 128), bf16),
            pltpu.VMEM((PART * PARTS, 128), bf16),
            pltpu.VMEM((C, C), bf16),
            pltpu.VMEM((C, 2 * C), bf16),
            pltpu.VMEM((C, C), bf16),
            pltpu.VMEM((3, C, 2 * C), bf16),
            pltpu.VMEM((2, 2560, C), bf16),
            pltpu.VMEM((2, 2560, C + 128), bf16),
            pltpu.VMEM((2, 3 * W, C), bf16),
            pltpu.VMEM((2, 3 * W, C + 128), f32),
            pltpu.VMEM((2, 3 * W, 128), f32),
            pltpu.VMEM((2, W, C), bf16),
            pltpu.VMEM((4 * W, 3 * C), bf16),
            pltpu.VMEM((9 * C, 3 * C), bf16),
            pltpu.VMEM((2 * W, 3 * C), f32),
            pltpu.VMEM((4 * W, C), bf16),
            pltpu.VMEM((2 * W, C), bf16),
            pltpu.SemaphoreType.DMA((162,)),
            pltpu.SemaphoreType.DMA((96,)),
            pltpu.SemaphoreType.DMA((32,)),
            pltpu.SemaphoreType.DMA((32,)),
            pltpu.SemaphoreType.DMA((16,)),
            pltpu.SemaphoreType.DMA((11,)),
        ],
        compiler_params=pltpu.CompilerParams(
            collective_id=0, has_side_effects=True, vmem_limit_bytes=60 * 1024 * 1024),
    )(latent_features.reshape(2 * W, C), conv_weight.reshape(648, C), attn_gain, unit_gain,
      w_query, w_key, w_value, w_proj, upsample_weight)
    return out.astype(bf16).reshape(4, 1, W, C)


def solution(mesh):
    in_specs = (P("tm", "rows", None, None), P(), P(), P(), P(), P(), P(), P(None, None, None, "rows", None), P())
    return jax.shard_map(body, mesh=mesh, in_specs=in_specs, out_specs=P("tm", "rows", None, None), check_vma=False)
```

```python
import math

import jax
import jax.numpy as jnp
from jax import lax
from jax.experimental import pallas as pl
from jax.experimental.pallas import tpu as pltpu
from jax.sharding import PartitionSpec as P

epsilon = 1e-06
MESH = pl.DeviceIdType.MESH
C = 384
W = 160
PART = 256
HALF = 128
PARTS = 8
BLOCK = 672
SCALE = math.log2(math.e) / math.sqrt(C)

PLACE = (0, 2, 3, 1)
STEPS = (
    ((
        ("zo", "part"), ("xo", "part"), ("xo", 1), ("zo", 1), ("X", "part", 0, 3, 0), ("X", "part", 0, 1, 0),
        ("X", "part", 0, 3, 1), ("X", "part", 0, 1, 1), ("X", 1, 0, 3, 0), ("X", 1, 0, 1, 0), ("Z", "part", 3, 0),
        ("Z", "part", 1, 1), ("X", 1, 0, 3, 1), ("X", 1, 0, 1, 1), ("X", "part", 0, 2, 0), ("X", "part", 0, 2, 1),
        ("YO", 0), ("Z", "part", 3, 1), ("Z", "part", 1, 0), ("xo", 0), ("X", 1, 0, 2, 0), ("X", "part", 3, 1, 0),
        ("X", "part", 3, 3, 0), ("X", "part", 1, 1, 1), ("X", "part", 1, 3, 1), ("X", "part", 3, 3, 1),
        ("X", 1, 0, 2, 1),
    ), (
        ("zo", "part"), ("xo", "part"), ("xo", 1), ("X", "part", 0, 3, 0), ("X", "part", 0, 1, 0),
        ("X", "part", 0, 3, 1), ("X", "part", 0, 1, 1), ("X", 1, 0, 3, 0), ("X", 1, 0, 1, 0), ("X", 1, 0, 3, 1),
        ("X", 1, 0, 1, 1), ("X", "part", 0, 2, 0), ("X", "part", 0, 2, 1), ("YO", 0), ("X", 1, 0, 2, 0),
        ("Z", "part", 3, 0), ("Z", "part", 1, 1), ("zo", 1), ("X", 1, 0, 2, 1),
    ), ("pr", 1, 0)),
    ((
        ("X", "part", 1, 3, 0), ("X", "part", 3, 1, 1), ("Y", 0, 3, 0), ("Y", 0, 1, 1), ("X", "part", 1, 1, 0),
        ("X", 0, 0, 3, 0), ("Z", 1, 3, 0), ("Z", 1, 1, 1), ("zo", 0), ("X", 0, 0, 1, 0), ("X", 0, 0, 3, 1),
        ("X", "part", 3, 2, 0), ("Y", 0, 3, 1), ("Y", 0, 1, 0), ("X", 0, 0, 1, 1), ("X", "part", 1, 2, 0),
        ("X", "part", 1, 2, 1), ("YO", 1), ("Z", 1, 3, 1), ("Z", 1, 1, 0), ("X", "part", 3, 2, 1), ("YO", 3),
        ("X", 0, 0, 2, 0), ("Z", "part", 2, 0), ("Z", "part", 2, 1), ("Y", 0, 2, 0), ("Y", 0, 2, 1),
        ("X", 1, 3, 1, 0), ("X", 1, 3, 3, 0), ("X", 1, 1, 1, 1), ("X", 1, 1, 3, 1), ("X", 0, 0, 2, 1),
        ("Y", 1, 3, 0), ("Y", 1, 1, 1), ("X", 1, 3, 3, 1), ("X", 1, 3, 1, 1), ("X", 1, 1, 3, 0),
        ("X", "part", 2, 3, 0), ("X", 1, 1, 1, 0), ("Y", 1, 3, 1), ("Y", 1, 1, 0), ("X", "part", 2, 3, 1),
        ("X", "part", 2, 1, 0), ("X", "part", 2, 1, 1), ("X", 1, 3, 2, 0), ("X", 1, 1, 2, 1), ("Y", 3, 3, 0),
        ("X", 1, 1, 2, 0), ("Y", 3, 1, 1),
    ), (
        ("Z", "part", 3, 1), ("Z", "part", 1, 0), ("xo", 0), ("X", "part", 3, 3, 0), ("X", "part", 3, 1, 0),
        ("Y", 0, 3, 0), ("Y", 0, 1, 1), ("X", "part", 1, 3, 1), ("X", "part", 1, 1, 1), ("X", "part", 3, 1, 1),
        ("X", "part", 3, 3, 1), ("X", "part", 1, 1, 0), ("X", "part", 1, 3, 0), ("Y", 0, 3, 1), ("Y", 0, 1, 0),
        ("X", 0, 0, 1, 0), ("X", 0, 0, 3, 0), ("X", 0, 0, 1, 1), ("X", 0, 0, 3, 1), ("X", "part", 1, 2, 1),
        ("X", "part", 3, 2, 0), ("Y", 0, 2, 0), ("Y", 0, 2, 1), ("X", "part", 3, 2, 1), ("YO", 3),
        ("X", "part", 1, 2, 0), ("YO", 1), ("Z", "part", 2, 0), ("Z", "part", 2, 1), ("X", 0, 0, 2, 0),
        ("X", 0, 0, 2, 1), ("X", "part", 2, 3, 0), ("Z", 1, 3, 0), ("X", "part", 2, 1, 0), ("Z", 1, 1, 1), ("zo", 0),
        ("X", "part", 2, 3, 1), ("X", "part", 2, 1, 1),
    ), ("un", 0)),
    ((
        ("Z", 1, 2, 0), ("Z", 1, 2, 1), ("X", "part", 2, 2, 0), ("X", 1, 3, 2, 1),
    ), (
        ("Y", 3, 3, 0), ("Y", 3, 1, 1),
    ), ("pr", 0, 0)),
    ((
        ("X", "part", 2, 2, 1), ("YO", 2), ("Y", 3, 3, 1), ("Y", 3, 1, 0),
    ), (
        ("X", "part", 2, 2, 0), ("Z", 1, 3, 1), ("Z", 1, 1, 0), ("X", 1, 3, 1, 0), ("X", 1, 3, 3, 0), ("Y", 3, 3, 1),
        ("Y", 3, 1, 0), ("X", 1, 1, 1, 1), ("X", 1, 1, 3, 1), ("X", "part", 2, 2, 1), ("YO", 2), ("X", 1, 3, 3, 1),
        ("X", 1, 3, 1, 1), ("Y", 1, 3, 0), ("Y", 1, 1, 1), ("X", 1, 1, 3, 0), ("X", 1, 1, 1, 0), ("X", 1, 3, 2, 0),
        ("X", 1, 1, 2, 1), ("Y", 1, 3, 1), ("Y", 1, 1, 0), ("X", 1, 3, 2, 1),
    ), ("pr", 1, 3)),
    ((
        ("Z", 0, 3, 0), ("Z", 0, 1, 1),
    ), (
        ("X", 1, 1, 2, 0),
    ), ("pr", 1, 1)),
    ((
        ("X", 1, 2, 3, 0), ("X", 1, 2, 1, 0),
    ), (
    ), ("ask", 1)),
    ((
        ("Y", 1, 2, 0), ("Y", 1, 2, 1), ("Z", 0, 3, 1), ("X", 1, 2, 3, 1), ("Z", 0, 1, 0), ("X", 1, 2, 1, 1),
    ), (
        ("Y", 3, 2, 0), ("Y", 3, 2, 1),
    ), ("at", 1, 0)),
    ((
        ("X", 0, 3, 3, 0), ("X", 0, 3, 1, 0),
    ), (
        ("Z", 1, 2, 0), ("Z", 1, 2, 1),
    ), ("at", 1, 1)),
    ((
        ("X", 0, 1, 3, 1), ("Y", 3, 2, 0), ("X", 0, 1, 1, 1), ("Y", 3, 2, 1), ("X", 1, 2, 2, 0), ("X", 0, 3, 1, 1),
        ("X", 0, 3, 3, 1), ("X", 0, 1, 1, 0), ("Y", 2, 3, 0), ("Y", 2, 1, 1), ("X", 0, 1, 3, 0), ("X", 1, 2, 2, 1),
    ), (
        ("Y", 2, 3, 0), ("Y", 2, 1, 1), ("Z", 0, 3, 0), ("Z", 0, 1, 1), ("X", 1, 2, 3, 0), ("X", 1, 2, 1, 0),
        ("Y", 2, 3, 1), ("Y", 2, 1, 0), ("Z", 0, 3, 1), ("Z", 0, 1, 0), ("X", 1, 2, 3, 1), ("X", 1, 2, 1, 1),
        ("X", 0, 3, 3, 0), ("X", 0, 3, 1, 0), ("Y", 1, 2, 0), ("Y", 1, 2, 1), ("X", 0, 1, 3, 1), ("X", 0, 1, 1, 1),
        ("X", 1, 2, 2, 0), ("X", 0, 3, 1, 1), ("Y", 2, 2, 0), ("Z", 0, 2, 0), ("Y", 2, 2, 1), ("Z", 0, 2, 1),
        ("X", 0, 3, 3, 1), ("X", 0, 1, 1, 0), ("X", 0, 1, 3, 0), ("X", 1, 2, 2, 1),
    ), ("pr", 1, 2)),
    ((
    ), (
    ), ("at", 1, 2)),
    ((
        ("X", 0, 3, 2, 0), ("X", 0, 1, 2, 1), ("Y", 2, 3, 1), ("Y", 2, 1, 0), ("X", 0, 3, 2, 1),
    ), (
        ("X", 0, 3, 2, 0), ("X", 0, 1, 2, 1),
    ), ("fin", 1)),
    ((
        ("X", 0, 1, 2, 0), ("Z", 0, 2, 0), ("Z", 0, 2, 1), ("Y", 2, 2, 0), ("Y", 2, 2, 1),
    ), (
        ("X", 0, 2, 3, 0), ("X", 0, 3, 2, 1), ("X", 0, 2, 3, 1), ("X", 0, 2, 1, 0),
    ), ("un", 3)),
    ((
    ), (
        ("X", 0, 1, 2, 0), ("X", 0, 2, 1, 1),
    ), ("pr", 0, 3)),
    ((
    ), (
    ), ("pr", 0, 1)),
    ((
        ("X", 0, 2, 3, 0), ("X", 0, 2, 1, 0),
    ), (
    ), ("ask", 0)),
    ((
        ("X", 0, 2, 3, 1), ("X", 0, 2, 1, 1),
    ), (
        ("X", 0, 2, 2, 0),
    ), ("at", 0, 0)),
    ((
    ), (
        ("X", 0, 2, 2, 1),
    ), ("un", 1)),
    ((
        ("X", 0, 2, 2, 0),
    ), (
    ), ("at", 0, 1)),
    ((
        ("X", 0, 2, 2, 1),
    ), (
    ), ("un", 2)),
    ((
    ), (
    ), ("cv", 0)),
    ((
    ), (
    ), ("pr", 0, 2)),
    ((
    ), (
    ), ("at", 0, 2)),
    ((
    ), (
    ), ("fin", 0)),
    ((
    ), (
    ), None),
)


def dot(left, right):
    return jnp.dot(left, right, preferred_element_type=jnp.float32)


def rms_scale(values, gain):
    widened = values.astype(jnp.float32)
    return widened * lax.rsqrt(jnp.mean(widened * widened, axis=-1, keepdims=True) + epsilon) * gain


def kernel(latent_hbm, shard_hbm, attn_gain_hbm, unit_gain_hbm, w_query_hbm, w_key_hbm, w_value_hbm, w_proj_hbm, upsample_hbm, out,
           latent, shard, attn_gain, unit_gain, cells, parts, packed, w_query, w_key_value, w_proj, upsample,
           keys, values, queries, numerator, row_max, attended, extended, conv_weight, sums, units, carried,
           send_sems, grid_sems, y_sems, core_sems, frame_sems, local_sems):
    tm, rows = lax.axis_index("tm"), lax.axis_index("rows")
    z, x = rows // 4, lax.rem(rows, 4)
    core = lax.rem(tm, 2)
    z_lo = lax.rem(tm // 2, 4)
    y = tm // 8

    def ring(value, step):
        return lax.rem(value + (step % 4), 4)

    def to_z(step):
        return {"tm": tm, "rows": ring(z, step) * 4 + x}

    def to_x(step):
        return {"tm": tm, "rows": z * 4 + ring(x, step)}

    def to_y(step):
        return {"tm": (ring(y, step) * 4 + z_lo) * 2 + core, "rows": rows}

    sibling = {"tm": tm + 1 - 2 * core, "rows": rows}
    later = {"tm": lax.rem(tm + 1, 32), "rows": rows}
    before = {"tm": lax.rem(tm + 31, 32), "rows": rows}
    targets = {("z", 1): to_z(1), ("z", -1): to_z(-1), ("x", 1): to_x(1), ("x", -1): to_x(-1),
               ("y", 1): to_y(1), ("y", -1): to_y(-1), ("core", 1): sibling, ("tm", 1): later}

    barrier = pltpu.get_barrier_semaphore()
    greeted = list(targets.values()) + [before]
    for target in greeted:
        pl.semaphore_signal(barrier, inc=1, device_id=target, device_id_type=MESH)

    loads = []
    for source, target in ((shard_hbm, shard), (latent_hbm, latent), (attn_gain_hbm, attn_gain),
                           (unit_gain_hbm, unit_gain), (w_key_hbm, w_key_value.at[:, pl.ds(0, C)]), (w_value_hbm, w_key_value.at[:, pl.ds(C, C)]), (w_query_hbm, w_query),
                           (w_proj_hbm, w_proj), (upsample_hbm, upsample)):
        load = pltpu.make_async_copy(source, target, local_sems.at[2 + len(loads)])
        load.start()
        loads.append(load)
    loads[0].wait()

    for n in range(3):
        packed[pl.ds(BLOCK * n, 640)] = shard[:640, 128 * n:128 * n + 128]
        packed[pl.ds(BLOCK * n + 640, 32)] = jnp.concatenate(
            [shard[640:648, 128 * n:128 * n + 128].astype(jnp.float32), jnp.zeros((24, 128), jnp.float32)],
            axis=0).astype(jnp.bfloat16)
    packed[pl.ds(BLOCK * 3, 32)] = jnp.zeros((32, 128), jnp.bfloat16)

    pl.semaphore_wait(barrier, len(greeted))

    sent = {}

    def slot(dz, dx):
        return ring(z, dz) * 4 + ring(x, dx)

    def cell_unit(frame):
        return lambda dz, dx, h: cells.at[slot(dz, dx), pl.ds(W * frame + W // 2 * h, W // 2)]

    def part_unit(dz, dx, h):
        return parts.at[slot(dz, dx), pl.ds(PART * (core * 4 + y) + HALF * h, HALF)]

    def y_unit(dz, dy, h):
        return parts.at[pl.ds(4 * ring(z, dz), 4), pl.ds(PART * (core * 4 + ring(y, dy)) + HALF * h, HALF)]

    def push(tag, where, parts_of):
        index = sent.setdefault(tag, (len(sent), where, parts_of))[0]
        started(index, where, parts_of).start()

    def started(index, where, parts_of):
        source, target, recv_sem = parts_of()
        return pltpu.make_async_remote_copy(
            src_ref=source, dst_ref=target, send_sem=send_sems.at[index], recv_sem=recv_sem,
            device_id=targets[where], device_id_type=MESH)

    def arrive(region, recv_sem):
        pltpu.make_async_remote_copy(
            src_ref=region, dst_ref=region, send_sem=send_sems.at[0], recv_sem=recv_sem,
            device_id=sibling, device_id_type=MESH).wait_recv()

    grid_kinds = {"part": (part_unit, 0), 0: (cell_unit(0), 32), 1: (cell_unit(1), 64)}

    def grid_sem(kind, dz, dx, h):
        return grid_sems.at[grid_kinds[kind][1] + ((dz % 4) * 4 + dx % 4) * 2 + h]

    def grid_push(kind, dz, dx, h, axis, step, from_own=False):
        def parts_of():
            unit = grid_kinds[kind][0](dz, dx, h)
            sem = grid_sem(kind, dz - step, dx, h) if axis == "z" else grid_sem(kind, dz, dx - step, h)
            return own(kind, h) if from_own else unit, unit, sem

        push((kind, dz, dx, h, axis, step), (axis, step), parts_of)

    def grid_arrive(kind, dz, dx, h):
        arrive(grid_kinds[kind][0](dz, dx, h), grid_sem(kind, dz, dx, h))

    def y_sem(dz, dy, h):
        return y_sems.at[((dz % 4) * 4 + dy % 4) * 2 + h]

    def y_push(dz, dy, h, step):
        push(("y", dz, dy, h, step), ("y", step),
             lambda: (y_unit(dz, dy, h), y_unit(dz, dy, h), y_sem(dz, dy - step, h)))

    def y_arrive(dz, dy, h):
        arrive(y_unit(dz, dy, h), y_sem(dz, dy, h))

    def own(kind, h):
        if kind == "part":
            return packed.at[pl.ds(PART * (core * 4 + y) + HALF * h, HALF)]
        return latent.at[pl.ds(W * kind + W // 2 * h, W // 2)]

    ways = ((0, 1), (1, -1), (1, 1), (0, -1))
    forwarded = {(3, 0): 1, (1, 1): -1}

    def z_own(kind):
        for h, step in ways:
            grid_push(kind, 0, 0, h, "z", step, True)

    def x_out(kind, dz, h, from_own=False):
        first = 1 if h == 0 else -1
        grid_push(kind, dz, 0, h, "x", first, from_own)
        grid_push(kind, dz, 0, h, "x", -first, from_own)

    def x_own(kind):
        for h in range(2):
            x_out(kind, 0, h, True)

    def z_arrival(kind, dz, h):
        grid_arrive(kind, dz, 0, h)
        if (dz, h) in forwarded:
            grid_push(kind, dz, 0, h, "z", forwarded[dz, h])
        x_out(kind, dz, h)

    def x_arrival(kind, dz, dx, h):
        grid_arrive(kind, dz, dx, h)
        if (dx, h) in forwarded:
            grid_push(kind, dz, dx, h, "x", forwarded[dx, h])

    def y_own(dz):
        for h, step in ways:
            y_push(dz, 0, h, step)
        for h in range(2):
            core_push(dz, 0, h)

    def y_arrival(dz, dy, h):
        y_arrive(dz, dy, h)
        if (dy, h) in forwarded:
            y_push(dz, dy, h, forwarded[dy, h])
        core_push(dz, dy, h)

    def core_unit(dz, dy, h, which):
        return parts.at[pl.ds(4 * ring(z, dz), 4), pl.ds(PART * (which * 4 + ring(y, dy)) + HALF * h, HALF)]

    def core_sem(dz, dy, h):
        return core_sems.at[((dz % 4) * 4 + dy % 4) * 2 + h]

    def core_push(dz, dy, h):
        push(("core", dz, dy, h), ("core", 1),
             lambda: (core_unit(dz, dy, h, core), core_unit(dz, dy, h, core), core_sem(dz, dy, h)))

    def unpack(dz):
        for dy in range(4):
            for h in range(2):
                arrive(core_unit(dz, dy, h, 1 - core), core_sem(dz, dy, h))
        group = ring(z, dz)
        row = pl.multiple_of(96 * group, 32)

        def taps(loaded, first, count):
            for n in range(3):
                for i in range(3 * count):
                    target = pl.ds(pl.multiple_of(C * (first + i // 3) + row, 32), 96)
                    lanes = slice(C * (i % 3) + 128 * n, C * (i % 3) + 128 * n + 128)
                    conv_weight[target, lanes] = loaded[n][:, i].reshape(96, 128).astype(jnp.bfloat16)

        def load(n, start, count):
            block = parts[pl.ds(4 * group, 4), pl.ds(pl.multiple_of(BLOCK * n + start, 16), count)]
            return block.astype(jnp.float32).reshape(4, count // 24, 24, 128)

        def pair(j, carry):
            taps([load(n, 144 * j, 144) for n in range(3)], 2 * j, 2)
            return carry

        lax.fori_loop(0, 4, pair, 0)
        taps([load(n, 576, 96) for n in range(3)], 8, 1)

    def gained(ref):
        return ref[...].reshape(1, C)

    def project(frame, dz):
        if (frame, dz) == (1, 0):
            for load in loads[2:]:
                load.wait()
        group = ring(z, dz)

        def one(i, carry):
            block = cells[pl.ds(4 * group + 2 * i, 2), pl.ds(W * frame, W)].reshape(2 * W, C)
            normed = rms_scale(block, gained(attn_gain)).astype(jnp.bfloat16)
            place = pl.ds(pl.multiple_of(640 * PLACE[dz] + 2 * W * i, 64), 2 * W)
            both = dot(normed, w_key_value[...]).astype(jnp.bfloat16)
            keys[frame, place] = both[:, :C]
            values[frame, place, 0:C] = both[:, C:]
            return carry

        lax.fori_loop(0, 2, one, 0)

    def ask(frame):
        block = jnp.concatenate([cells[lax.rem(rows + 15 + b, 16), pl.ds(W * frame, W)] for b in range(3)], axis=0)
        normed = rms_scale(block, gained(attn_gain)).astype(jnp.bfloat16)
        queries[frame] = dot(normed, w_query[...]).astype(jnp.bfloat16)

    def attend(h, step):
        asked = (slice(0, 240), slice(240, 480), slice(0, 480))[step]
        place = slice(1920, 2560) if step == 2 else slice(0, 1920)
        scores = lax.dot_general(queries[h, asked], keys[h, place], (((1,), (1,)), ((), ())),
                                 preferred_element_type=jnp.float32)
        top = jnp.max(scores, axis=-1, keepdims=True)
        if step == 2:
            old = row_max[h][:, :1]
            top = jnp.maximum(top, old)
            rescale = jnp.exp2((old - top) * SCALE)
        weights = jnp.exp2((scores - top) * SCALE).astype(jnp.bfloat16)
        added = dot(weights, values[h, place])
        if step == 2:
            numerator[h] = numerator[h] * rescale + added
        else:
            numerator[h, asked] = added
            row_max[h, asked] = jnp.broadcast_to(top, (240, 128))

    def finish(h):
        scale = 1.0 / numerator[h, :, C:]
        mixed = jnp.concatenate(
            [numerator[h, :, 128 * n:128 * n + 128] * scale for n in range(3)], axis=-1).astype(jnp.bfloat16)
        projected = dot(mixed, w_proj[...])
        for b in range(3):
            here = cells[lax.rem(rows + 15 + b, 16), pl.ds(W * h, W)].astype(jnp.float32)
            summed = (here + projected[W * b:W * b + W]).astype(jnp.bfloat16)
            if b == 1:
                attended[h] = summed
            scaled = rms_scale(summed, gained(unit_gain))
            activated = scaled / (1.0 + jnp.exp(-scaled))
            inside = jnp.logical_and(rows + b >= 1, rows + b <= 16)
            extended[pl.ds(W * h, W), C * b:C * b + C] = jnp.where(inside, activated, 0.0).astype(jnp.bfloat16)

    def earlier(block):
        return jnp.where(tm > 0, block, jnp.zeros_like(block))

    def convolve(a, source, frames):
        return dot(extended[pl.ds(W * (source - 2), W * frames)], conv_weight[pl.ds(3 * C * a, 3 * C)])

    column = lax.broadcasted_iota(jnp.int32, (W, C), 0)

    def joined(total):
        left = pltpu.roll(total[:, :C], 1, 0)
        right = pltpu.roll(total[:, 2 * C:], W - 1, 0)
        return total[:, C:2 * C] + jnp.where(column > 0, left, 0.0) + jnp.where(column < W - 1, right, 0.0)

    def carried_half(place, half):
        return carried.at[pl.ds(W * place + W // 2 * half, W // 2)]

    def carry(h, total):
        carried[pl.ds(W * (2 + h), W)] = joined(total).astype(jnp.bfloat16)
        for half in range(2):
            push(("carried", h, half), ("tm", 1), lambda half=half: (
                carried_half(2 + h, half), carried_half(h, half), frame_sems.at[2 * h + half]))

    def brought(h):
        for half in range(2):
            arrive(carried_half(h, half), frame_sems.at[2 * h + half])
        return earlier(carried[pl.ds(W * h, W)]).astype(jnp.float32)

    def early_convolve(number):
        sums[pl.ds(0, W)] = convolve(1, 3, 1)
        carry(1, convolve(0, 3, 1))

    loads[1].wait()
    own_slice = pl.ds(pl.multiple_of(PART * (core * 4 + y), PART), PART)
    parts[rows, own_slice] = packed[own_slice]
    cells[rows] = latent[...]
    values[:, :, C:] = jnp.ones((2, 2560, 128), jnp.bfloat16)
    actions = {"zo": z_own, "xo": x_own, "Z": z_arrival, "X": x_arrival, "Y": y_arrival, "YO": y_own,
               "pr": project, "ask": ask, "at": attend, "fin": finish, "un": unpack, "cv": early_convolve}

    def perform(operations):
        for name, *operands in operations:
            actions[name](*operands)

    for ahead, behind, work in STEPS:
        common = 0
        while common < min(len(ahead), len(behind)) and ahead[common] == behind[common]:
            common += 1
        perform(ahead[:common])
        if len(ahead) > common:
            pl.when(z_lo == 3)(lambda: perform(ahead[common:]))
        if len(behind) > common:
            pl.when(z_lo < 3)(lambda: perform(behind[common:]))
        if work is not None:
            perform((work,))

    carry(0, sums[pl.ds(0, W)] + convolve(0, 2, 1))

    def unit_half(frame, half):
        return units.at[pl.ds(W * frame + W // 2 * half, W // 2)]

    def unit(h, convolved):
        units[pl.ds(W * (2 + h), W)] = (attended[h].astype(jnp.float32) + convolved).astype(jnp.bfloat16)
        for half in range(2):
            push(("unit", h, half), ("tm", 1), lambda half=half: (
                unit_half(2 + h, half), unit_half(h, half), frame_sems.at[4 + 2 * h + half]))

    def earlier_unit(h):
        for half in range(2):
            arrive(unit_half(h, half), frame_sems.at[4 + 2 * h + half])
        return earlier(units[pl.ds(W * h, W)])

    def put(h, stretched):
        out[2 * h] = stretched[:, :C]
        out[2 * h + 1] = stretched[:, C:]

    sums[...] = convolve(2, 2, 2)
    sums[pl.ds(W, W)] += convolve(1, 2, 1)
    unit(1, joined(sums[pl.ds(W, W)]) + brought(1))
    convolved = joined(sums[pl.ds(0, W)])
    last = dot(units[pl.ds(W * 3, W)], upsample[2])
    unit(0, convolved + brought(0))
    newest = units[pl.ds(W * 2, W)]
    last = last + dot(newest, upsample[1])
    first = dot(newest, upsample[2])
    newest = earlier_unit(1)
    put(1, last + dot(newest, upsample[0]))
    first = first + dot(newest, upsample[1])
    put(0, first + dot(earlier_unit(0), upsample[0]))
    for entry in sent.values():
        started(*entry).wait_send()


def body(latent_features, attn_gain, w_query, w_key, w_value, w_proj, unit_gain, conv_weight, upsample_weight):
    vmem = pl.BlockSpec(memory_space=pltpu.VMEM)
    hbm = pl.BlockSpec(memory_space=pltpu.HBM)
    bf16, f32 = jnp.bfloat16, jnp.float32
    out = pl.pallas_call(
        kernel,
        out_shape=jax.ShapeDtypeStruct((4, W, C), f32),
        in_specs=[hbm] * 9,
        out_specs=vmem,
        scratch_shapes=[
            pltpu.VMEM((2 * W, C), bf16),
            pltpu.VMEM((648, C), bf16),
            pltpu.VMEM((C,), f32),
            pltpu.VMEM((C,), f32),
            pltpu.VMEM((16, 2 * W, C), bf16),
            pltpu.VMEM((16, PART * PARTS, 128), bf16),
            pltpu.VMEM((PART * PARTS, 128), bf16),
            pltpu.VMEM((C, C), bf16),
            pltpu.VMEM((C, 2 * C), bf16),
            pltpu.VMEM((C, C), bf16),
            pltpu.VMEM((3, C, 2 * C), bf16),
            pltpu.VMEM((2, 2560, C), bf16),
            pltpu.VMEM((2, 2560, C + 128), bf16),
            pltpu.VMEM((2, 3 * W, C), bf16),
            pltpu.VMEM((2, 3 * W, C + 128), f32),
            pltpu.VMEM((2, 3 * W, 128), f32),
            pltpu.VMEM((2, W, C), bf16),
            pltpu.VMEM((2 * W, 3 * C), bf16),
            pltpu.VMEM((9 * C, 3 * C), bf16),
            pltpu.VMEM((2 * W, 3 * C), f32),
            pltpu.VMEM((4 * W, C), bf16),
            pltpu.VMEM((4 * W, C), bf16),
            pltpu.SemaphoreType.DMA((154,)),
            pltpu.SemaphoreType.DMA((96,)),
            pltpu.SemaphoreType.DMA((32,)),
            pltpu.SemaphoreType.DMA((32,)),
            pltpu.SemaphoreType.DMA((8,)),
            pltpu.SemaphoreType.DMA((11,)),
        ],
        compiler_params=pltpu.CompilerParams(
            collective_id=0, has_side_effects=True, vmem_limit_bytes=60 * 1024 * 1024),
    )(latent_features.reshape(2 * W, C), conv_weight.reshape(648, C), attn_gain, unit_gain,
      w_query, w_key, w_value, w_proj, upsample_weight)
    return out.astype(bf16).reshape(4, 1, W, C)


def solution(mesh):
    in_specs = (P("tm", "rows", None, None), P(), P(), P(), P(), P(), P(), P(None, None, None, "rows", None), P())
    return jax.shard_map(body, mesh=mesh, in_specs=in_specs, out_specs=P("tm", "rows", None, None), check_vma=False)
```

```python
import math

import jax
import jax.numpy as jnp
from jax import lax
from jax.experimental import pallas as pl
from jax.experimental.pallas import tpu as pltpu
from jax.sharding import PartitionSpec as P

epsilon = 1e-06
MESH = pl.DeviceIdType.MESH
C = 384
W = 160
PART = 256
HALF = 128
PARTS = 8
BLOCK = 672
SCALE = math.log2(math.e) / math.sqrt(C)

PLACE = (0, 2, 3, 1)
STEPS = (
    ((
        ("zo", "part"), ("xo", "part"), ("xo", 1), ("zo", 1), ("X", "part", 0, 3, 0), ("X", "part", 0, 1, 0),
        ("X", "part", 0, 3, 1), ("X", "part", 0, 1, 1), ("X", 1, 0, 3, 0), ("X", 1, 0, 1, 0), ("Z", "part", 3, 0),
        ("Z", "part", 1, 1), ("Z", "part", 3, 1), ("Z", "part", 1, 0), ("xo", 0), ("X", 1, 0, 3, 1),
        ("X", 1, 0, 1, 1), ("X", "part", 0, 2, 0), ("X", "part", 0, 2, 1), ("YO", 0), ("X", "part", 3, 1, 0),
        ("X", 1, 0, 2, 0), ("X", "part", 1, 1, 1), ("X", "part", 3, 3, 0), ("X", "part", 3, 1, 1),
        ("X", "part", 1, 3, 1), ("X", "part", 1, 1, 0), ("X", "part", 3, 3, 1), ("X", "part", 1, 3, 0),
        ("X", 0, 0, 1, 0), ("Z", 1, 3, 0), ("Z", 1, 1, 1), ("zo", 0), ("Y", 0, 3, 0), ("Y", 0, 1, 1),
        ("X", 0, 0, 3, 0), ("X", 0, 0, 1, 1), ("Z", 1, 3, 1), ("Z", 1, 1, 0), ("Z", "part", 2, 0),
        ("Z", "part", 2, 1), ("X", 0, 0, 3, 1), ("X", 1, 0, 2, 1),
    ), (
        ("zo", "part"), ("xo", "part"), ("xo", 1), ("X", "part", 0, 3, 0), ("X", "part", 0, 1, 0),
        ("X", "part", 0, 3, 1), ("X", "part", 0, 1, 1), ("X", 1, 0, 3, 0), ("X", 1, 0, 1, 0), ("X", 1, 0, 3, 1),
        ("X", 1, 0, 1, 1), ("X", "part", 0, 2, 0), ("X", "part", 0, 2, 1), ("YO", 0), ("Z", "part", 3, 0),
        ("Z", "part", 1, 1), ("zo", 1), ("X", 1, 0, 2, 0), ("X", 1, 0, 2, 1),
    ), ("pr", 1, 0)),
    ((
        ("Y", 0, 3, 1), ("X", "part", 3, 2, 0), ("Y", 0, 1, 0), ("X", "part", 1, 2, 1), ("X", "part", 1, 2, 0),
        ("YO", 1), ("X", "part", 3, 2, 1), ("YO", 3), ("X", 1, 3, 3, 0), ("X", 1, 3, 1, 0), ("Y", 0, 2, 0),
        ("Y", 0, 2, 1), ("X", 1, 1, 3, 1), ("X", 1, 1, 1, 1), ("X", 0, 0, 2, 0), ("X", 0, 0, 2, 1), ("Y", 1, 3, 0),
        ("Y", 1, 1, 1), ("X", 1, 3, 3, 1), ("X", 1, 3, 1, 1), ("X", 1, 1, 3, 0), ("X", 1, 1, 1, 0),
        ("X", "part", 2, 3, 0), ("X", "part", 2, 1, 0), ("Y", 1, 3, 1), ("Y", 1, 1, 0), ("X", "part", 2, 3, 1),
        ("X", "part", 2, 1, 1), ("X", 1, 3, 2, 0), ("X", 1, 1, 2, 1), ("Z", 1, 2, 0), ("Z", 1, 2, 1), ("Y", 3, 3, 0),
        ("Y", 3, 1, 1), ("X", 1, 1, 2, 0), ("X", 1, 3, 2, 1),
    ), (
        ("Z", "part", 3, 1), ("Z", "part", 1, 0), ("xo", 0), ("X", "part", 3, 3, 0), ("X", "part", 3, 1, 0),
        ("X", "part", 1, 3, 1), ("X", "part", 1, 1, 1), ("Y", 0, 3, 0), ("Y", 0, 1, 1), ("X", "part", 3, 1, 1),
        ("X", "part", 3, 3, 1), ("X", "part", 1, 1, 0), ("X", "part", 1, 3, 0), ("Y", 0, 3, 1), ("Y", 0, 1, 0),
        ("X", 0, 0, 1, 0), ("X", 0, 0, 3, 0), ("Z", "part", 2, 0), ("Z", "part", 2, 1), ("X", 0, 0, 1, 1),
        ("X", 0, 0, 3, 1), ("X", "part", 1, 2, 1), ("X", "part", 3, 2, 0), ("Y", 0, 2, 0), ("Y", 0, 2, 1),
        ("X", "part", 3, 2, 1), ("YO", 3), ("X", "part", 1, 2, 0), ("YO", 1), ("X", "part", 2, 1, 0),
        ("X", 0, 0, 2, 0), ("X", "part", 2, 1, 1), ("X", "part", 2, 3, 0), ("Z", 1, 3, 0), ("Z", 1, 1, 1), ("zo", 0),
        ("X", 0, 0, 2, 1), ("X", "part", 2, 3, 1),
    ), ("un", 0)),
    ((
        ("Z", 0, 3, 0), ("Z", 0, 1, 1), ("X", "part", 2, 2, 0), ("X", "part", 2, 2, 1), ("YO", 2), ("Z", 0, 3, 1),
        ("Z", 0, 1, 0), ("X", 1, 2, 3, 0), ("X", 1, 2, 1, 0),
    ), (
        ("X", "part", 2, 2, 1), ("X", "part", 2, 2, 0), ("YO", 2), ("Y", 3, 3, 0), ("Y", 3, 1, 1),
    ), ("pr", 0, 0)),
    ((
        ("Y", 3, 3, 1), ("Y", 3, 1, 0),
    ), (
        ("X", 1, 3, 1, 0), ("X", 1, 3, 3, 0), ("Z", 1, 3, 1), ("Z", 1, 1, 0), ("X", 1, 1, 1, 1), ("X", 1, 1, 3, 1),
        ("Y", 3, 3, 1), ("Y", 3, 1, 0), ("X", 1, 3, 2, 0), ("X", 1, 3, 1, 1), ("Y", 1, 3, 0), ("Y", 1, 1, 1),
        ("X", 1, 3, 3, 1), ("X", 1, 1, 1, 0), ("X", 1, 1, 3, 0), ("X", 1, 1, 2, 1), ("Y", 1, 3, 1), ("Y", 1, 1, 0),
        ("X", 1, 3, 2, 1),
    ), ("pr", 1, 3)),
    ((
        ("X", 1, 2, 3, 1), ("X", 1, 2, 1, 1),
    ), (
        ("Z", 1, 2, 0), ("Z", 1, 2, 1), ("X", 1, 1, 2, 0),
    ), ("pr", 1, 1)),
    ((
        ("X", 0, 3, 3, 0), ("X", 0, 3, 1, 0),
    ), (
    ), ("ask", 1)),
    ((
        ("Y", 1, 2, 0), ("Y", 1, 2, 1),
    ), (
        ("Y", 2, 3, 0), ("Y", 2, 1, 1),
    ), ("at", 1, 0)),
    ((
        ("X", 0, 1, 3, 1), ("X", 0, 1, 1, 1), ("X", 0, 3, 3, 1), ("X", 0, 3, 1, 1),
    ), (
        ("X", 1, 2, 3, 0), ("X", 1, 2, 1, 0), ("Z", 0, 3, 0), ("Z", 0, 1, 1),
    ), ("at", 1, 1)),
    ((
        ("Y", 3, 2, 0), ("Y", 3, 2, 1), ("X", 0, 1, 3, 0), ("X", 0, 1, 1, 0), ("X", 1, 2, 2, 0), ("X", 1, 2, 2, 1),
    ), (
        ("X", 1, 2, 3, 1), ("X", 1, 2, 1, 1), ("Y", 2, 3, 1), ("Y", 2, 1, 0), ("X", 1, 2, 2, 0), ("X", 0, 3, 1, 0),
        ("Y", 3, 2, 0), ("Y", 3, 2, 1), ("Z", 0, 3, 1), ("Z", 0, 1, 0), ("X", 0, 3, 3, 0), ("X", 0, 1, 1, 1),
        ("X", 0, 1, 3, 1), ("X", 1, 2, 2, 1),
    ), ("pr", 1, 2)),
    ((
    ), (
        ("Y", 1, 2, 0), ("Y", 1, 2, 1),
    ), ("at", 1, 2)),
    ((
        ("Y", 2, 3, 0), ("Y", 2, 1, 1), ("X", 0, 3, 2, 0), ("X", 0, 1, 2, 1), ("X", 0, 1, 2, 0), ("X", 0, 3, 2, 1),
    ), (
        ("X", 0, 3, 3, 1), ("X", 0, 3, 1, 1), ("X", 0, 1, 3, 0), ("X", 0, 1, 1, 0),
    ), ("fin", 1)),
    ((
        ("Y", 2, 3, 1), ("Y", 2, 1, 0), ("Z", 0, 2, 0), ("Z", 0, 2, 1), ("Y", 2, 2, 0), ("Y", 2, 2, 1),
        ("X", 0, 2, 3, 0), ("X", 0, 2, 1, 0),
    ), (
        ("Y", 2, 2, 0), ("Y", 2, 2, 1), ("Z", 0, 2, 0), ("Z", 0, 2, 1), ("X", 0, 3, 2, 0), ("X", 0, 1, 2, 1),
    ), ("un", 3)),
    ((
    ), (
        ("X", 0, 3, 2, 1), ("X", 0, 1, 2, 0),
    ), ("pr", 0, 3)),
    ((
        ("X", 0, 2, 3, 1), ("X", 0, 2, 1, 1),
    ), (
    ), ("pr", 0, 1)),
    ((
    ), (
        ("X", 0, 2, 3, 0), ("X", 0, 2, 1, 0),
    ), ("ask", 0)),
    ((
        ("X", 0, 2, 2, 0),
    ), (
    ), ("at", 0, 0)),
    ((
    ), (
        ("X", 0, 2, 3, 1), ("X", 0, 2, 1, 1),
    ), ("un", 1)),
    ((
        ("X", 0, 2, 2, 1),
    ), (
        ("X", 0, 2, 2, 0),
    ), ("at", 0, 1)),
    ((
    ), (
    ), ("un", 2)),
    ((
    ), (
        ("X", 0, 2, 2, 1),
    ), ("cv", 0)),
    ((
    ), (
    ), ("pr", 0, 2)),
    ((
    ), (
    ), ("at", 0, 2)),
    ((
    ), (
    ), ("fin", 0)),
    ((
    ), (
    ), None),
)


def dot(left, right):
    return jnp.dot(left, right, preferred_element_type=jnp.float32)


def rms_scale(values, gain):
    widened = values.astype(jnp.float32)
    return widened * lax.rsqrt(jnp.mean(widened * widened, axis=-1, keepdims=True) + epsilon) * gain


def kernel(latent_hbm, shard_hbm, attn_gain_hbm, unit_gain_hbm, w_query_hbm, w_key_hbm, w_value_hbm, w_proj_hbm, upsample_hbm, out,
           latent, shard, attn_gain, unit_gain, cells, parts, packed, w_query, w_key_value, w_proj, upsample,
           keys, values, queries, numerator, row_max, attended, extended, conv_weight, sums, units, carried,
           send_sems, grid_sems, y_sems, core_sems, frame_sems, local_sems):
    tm, rows = lax.axis_index("tm"), lax.axis_index("rows")
    z, x = rows // 4, lax.rem(rows, 4)
    core = lax.rem(tm, 2)
    z_lo = lax.rem(tm // 2, 4)
    y = tm // 8

    def ring(value, step):
        return lax.rem(value + (step % 4), 4)

    def to_z(step):
        return {"tm": tm, "rows": ring(z, step) * 4 + x}

    def to_x(step):
        return {"tm": tm, "rows": z * 4 + ring(x, step)}

    def to_y(step):
        return {"tm": (ring(y, step) * 4 + z_lo) * 2 + core, "rows": rows}

    sibling = {"tm": tm + 1 - 2 * core, "rows": rows}
    later = {"tm": lax.rem(tm + 1, 32), "rows": rows}
    before = {"tm": lax.rem(tm + 31, 32), "rows": rows}
    targets = {("z", 1): to_z(1), ("z", -1): to_z(-1), ("x", 1): to_x(1), ("x", -1): to_x(-1),
               ("y", 1): to_y(1), ("y", -1): to_y(-1), ("core", 1): sibling, ("tm", 1): later}

    barrier = pltpu.get_barrier_semaphore()
    greeted = list(targets.values()) + [before]
    for target in greeted:
        pl.semaphore_signal(barrier, inc=1, device_id=target, device_id_type=MESH)

    loads = []
    for source, target in ((shard_hbm, shard), (latent_hbm, latent), (attn_gain_hbm, attn_gain),
                           (unit_gain_hbm, unit_gain), (w_key_hbm, w_key_value.at[:, pl.ds(0, C)]), (w_value_hbm, w_key_value.at[:, pl.ds(C, C)]), (w_query_hbm, w_query),
                           (w_proj_hbm, w_proj), (upsample_hbm, upsample)):
        load = pltpu.make_async_copy(source, target, local_sems.at[2 + len(loads)])
        load.start()
        loads.append(load)
    loads[0].wait()

    for n in range(3):
        packed[pl.ds(BLOCK * n, 640)] = shard[:640, 128 * n:128 * n + 128]
        packed[pl.ds(BLOCK * n + 640, 32)] = jnp.concatenate(
            [shard[640:648, 128 * n:128 * n + 128].astype(jnp.float32), jnp.zeros((24, 128), jnp.float32)],
            axis=0).astype(jnp.bfloat16)
    packed[pl.ds(BLOCK * 3, 32)] = jnp.zeros((32, 128), jnp.bfloat16)

    pl.semaphore_wait(barrier, len(greeted))

    sent = {}

    def slot(dz, dx):
        return ring(z, dz) * 4 + ring(x, dx)

    def cell_unit(frame):
        return lambda dz, dx, h: cells.at[slot(dz, dx), pl.ds(W * frame + W // 2 * h, W // 2)]

    def part_unit(dz, dx, h):
        return parts.at[slot(dz, dx), pl.ds(PART * (core * 4 + y) + HALF * h, HALF)]

    def y_unit(dz, dy, h):
        return parts.at[pl.ds(4 * ring(z, dz), 4), pl.ds(PART * (core * 4 + ring(y, dy)) + HALF * h, HALF)]

    def push(tag, where, parts_of):
        index = sent.setdefault(tag, (len(sent), where, parts_of))[0]
        started(index, where, parts_of).start()

    def started(index, where, parts_of):
        source, target, recv_sem = parts_of()
        return pltpu.make_async_remote_copy(
            src_ref=source, dst_ref=target, send_sem=send_sems.at[index], recv_sem=recv_sem,
            device_id=targets[where], device_id_type=MESH)

    def arrive(region, recv_sem):
        pltpu.make_async_remote_copy(
            src_ref=region, dst_ref=region, send_sem=send_sems.at[0], recv_sem=recv_sem,
            device_id=sibling, device_id_type=MESH).wait_recv()

    grid_kinds = {"part": (part_unit, 0), 0: (cell_unit(0), 32), 1: (cell_unit(1), 64)}

    def grid_sem(kind, dz, dx, h):
        return grid_sems.at[grid_kinds[kind][1] + ((dz % 4) * 4 + dx % 4) * 2 + h]

    def grid_push(kind, dz, dx, h, axis, step, from_own=False):
        def parts_of():
            unit = grid_kinds[kind][0](dz, dx, h)
            sem = grid_sem(kind, dz - step, dx, h) if axis == "z" else grid_sem(kind, dz, dx - step, h)
            return own(kind, h) if from_own else unit, unit, sem

        push((kind, dz, dx, h, axis, step), (axis, step), parts_of)

    def grid_arrive(kind, dz, dx, h):
        arrive(grid_kinds[kind][0](dz, dx, h), grid_sem(kind, dz, dx, h))

    def y_sem(dz, dy, h):
        return y_sems.at[((dz % 4) * 4 + dy % 4) * 2 + h]

    def y_push(dz, dy, h, step):
        push(("y", dz, dy, h, step), ("y", step),
             lambda: (y_unit(dz, dy, h), y_unit(dz, dy, h), y_sem(dz, dy - step, h)))

    def y_arrive(dz, dy, h):
        arrive(y_unit(dz, dy, h), y_sem(dz, dy, h))

    def own(kind, h):
        if kind == "part":
            return packed.at[pl.ds(PART * (core * 4 + y) + HALF * h, HALF)]
        return latent.at[pl.ds(W * kind + W // 2 * h, W // 2)]

    ways = ((0, 1), (1, -1), (1, 1), (0, -1))
    forwarded = {(3, 0): 1, (1, 1): -1}

    def z_own(kind):
        for h, step in ways:
            grid_push(kind, 0, 0, h, "z", step, True)

    def x_out(kind, dz, h, from_own=False):
        first = 1 if h == 0 else -1
        grid_push(kind, dz, 0, h, "x", first, from_own)
        grid_push(kind, dz, 0, h, "x", -first, from_own)

    def x_own(kind):
        for h in range(2):
            x_out(kind, 0, h, True)

    def z_arrival(kind, dz, h):
        grid_arrive(kind, dz, 0, h)
        if (dz, h) in forwarded:
            grid_push(kind, dz, 0, h, "z", forwarded[dz, h])
        x_out(kind, dz, h)

    def x_arrival(kind, dz, dx, h):
        grid_arrive(kind, dz, dx, h)
        if (dx, h) in forwarded:
            grid_push(kind, dz, dx, h, "x", forwarded[dx, h])

    def y_own(dz):
        for h, step in ways:
            y_push(dz, 0, h, step)
        for h in range(2):
            core_push(dz, 0, h)

    def y_arrival(dz, dy, h):
        y_arrive(dz, dy, h)
        if (dy, h) in forwarded:
            y_push(dz, dy, h, forwarded[dy, h])
        core_push(dz, dy, h)

    def core_unit(dz, dy, h, which):
        return parts.at[pl.ds(4 * ring(z, dz), 4), pl.ds(PART * (which * 4 + ring(y, dy)) + HALF * h, HALF)]

    def core_sem(dz, dy, h):
        return core_sems.at[((dz % 4) * 4 + dy % 4) * 2 + h]

    def core_push(dz, dy, h):
        push(("core", dz, dy, h), ("core", 1),
             lambda: (core_unit(dz, dy, h, core), core_unit(dz, dy, h, core), core_sem(dz, dy, h)))

    def unpack(dz):
        for dy in range(4):
            for h in range(2):
                arrive(core_unit(dz, dy, h, 1 - core), core_sem(dz, dy, h))
        group = ring(z, dz)
        row = pl.multiple_of(96 * group, 32)

        def taps(loaded, first, count):
            for n in range(3):
                for i in range(3 * count):
                    target = pl.ds(pl.multiple_of(C * (first + i // 3) + row, 32), 96)
                    lanes = slice(C * (i % 3) + 128 * n, C * (i % 3) + 128 * n + 128)
                    conv_weight[target, lanes] = loaded[n][:, i].reshape(96, 128).astype(jnp.bfloat16)

        def load(n, start, count):
            block = parts[pl.ds(4 * group, 4), pl.ds(pl.multiple_of(BLOCK * n + start, 16), count)]
            return block.astype(jnp.float32).reshape(4, count // 24, 24, 128)

        def pair(j, carry):
            taps([load(n, 144 * j, 144) for n in range(3)], 2 * j, 2)
            return carry

        lax.fori_loop(0, 4, pair, 0)
        taps([load(n, 576, 96) for n in range(3)], 8, 1)

    def gained(ref):
        return ref[...].reshape(1, C)

    def project(frame, dz):
        if (frame, dz) == (1, 0):
            for load in loads[2:]:
                load.wait()
        group = ring(z, dz)

        def one(i, carry):
            block = cells[pl.ds(4 * group + 2 * i, 2), pl.ds(W * frame, W)].reshape(2 * W, C)
            normed = rms_scale(block, gained(attn_gain)).astype(jnp.bfloat16)
            place = pl.ds(pl.multiple_of(640 * PLACE[dz] + 2 * W * i, 64), 2 * W)
            both = dot(normed, w_key_value[...]).astype(jnp.bfloat16)
            keys[frame, place] = both[:, :C]
            values[frame, place, 0:C] = both[:, C:]
            return carry

        lax.fori_loop(0, 2, one, 0)

    def ask(frame):
        block = jnp.concatenate([cells[lax.rem(rows + 15 + b, 16), pl.ds(W * frame, W)] for b in range(3)], axis=0)
        normed = rms_scale(block, gained(attn_gain)).astype(jnp.bfloat16)
        queries[frame] = dot(normed, w_query[...]).astype(jnp.bfloat16)

    def attend(h, step):
        asked = (slice(0, 240), slice(240, 480), slice(0, 480))[step]
        place = slice(1920, 2560) if step == 2 else slice(0, 1920)
        scores = lax.dot_general(queries[h, asked], keys[h, place], (((1,), (1,)), ((), ())),
                                 preferred_element_type=jnp.float32)
        top = jnp.max(scores, axis=-1, keepdims=True)
        if step == 2:
            old = row_max[h][:, :1]
            top = jnp.maximum(top, old)
            rescale = jnp.exp2((old - top) * SCALE)
        weights = jnp.exp2((scores - top) * SCALE).astype(jnp.bfloat16)
        added = dot(weights, values[h, place])
        if step == 2:
            numerator[h] = numerator[h] * rescale + added
        else:
            numerator[h, asked] = added
            row_max[h, asked] = jnp.broadcast_to(top, (240, 128))

    def finish(h):
        scale = 1.0 / numerator[h, :, C:]
        mixed = jnp.concatenate(
            [numerator[h, :, 128 * n:128 * n + 128] * scale for n in range(3)], axis=-1).astype(jnp.bfloat16)
        projected = dot(mixed, w_proj[...])
        for b in range(3):
            here = cells[lax.rem(rows + 15 + b, 16), pl.ds(W * h, W)].astype(jnp.float32)
            summed = (here + projected[W * b:W * b + W]).astype(jnp.bfloat16)
            if b == 1:
                attended[h] = summed
            scaled = rms_scale(summed, gained(unit_gain))
            activated = scaled / (1.0 + jnp.exp(-scaled))
            inside = jnp.logical_and(rows + b >= 1, rows + b <= 16)
            extended[pl.ds(W * h, W), C * b:C * b + C] = jnp.where(inside, activated, 0.0).astype(jnp.bfloat16)

    def earlier(block):
        return jnp.where(tm > 0, block, jnp.zeros_like(block))

    def convolve(a, source, frames):
        return dot(extended[pl.ds(W * (source - 2), W * frames)], conv_weight[pl.ds(3 * C * a, 3 * C)])

    column = lax.broadcasted_iota(jnp.int32, (W, C), 0)

    def joined(total):
        left = pltpu.roll(total[:, :C], 1, 0)
        right = pltpu.roll(total[:, 2 * C:], W - 1, 0)
        return total[:, C:2 * C] + jnp.where(column > 0, left, 0.0) + jnp.where(column < W - 1, right, 0.0)

    def carried_half(place, half):
        return carried.at[pl.ds(W * place + W // 2 * half, W // 2)]

    def carry(h, total):
        carried[pl.ds(W * (2 + h), W)] = joined(total).astype(jnp.bfloat16)
        for half in range(2):
            push(("carried", h, half), ("tm", 1), lambda half=half: (
                carried_half(2 + h, half), carried_half(h, half), frame_sems.at[2 * h + half]))

    def brought(h):
        for half in range(2):
            arrive(carried_half(h, half), frame_sems.at[2 * h + half])
        return earlier(carried[pl.ds(W * h, W)]).astype(jnp.float32)

    def early_convolve(number):
        sums[pl.ds(0, W)] = convolve(1, 3, 1)
        carry(1, convolve(0, 3, 1))

    loads[1].wait()
    own_slice = pl.ds(pl.multiple_of(PART * (core * 4 + y), PART), PART)
    parts[rows, own_slice] = packed[own_slice]
    cells[rows] = latent[...]
    values[:, :, C:] = jnp.ones((2, 2560, 128), jnp.bfloat16)
    actions = {"zo": z_own, "xo": x_own, "Z": z_arrival, "X": x_arrival, "Y": y_arrival, "YO": y_own,
               "pr": project, "ask": ask, "at": attend, "fin": finish, "un": unpack, "cv": early_convolve}

    def perform(operations):
        for name, *operands in operations:
            actions[name](*operands)

    for ahead, behind, work in STEPS:
        common = 0
        while common < min(len(ahead), len(behind)) and ahead[common] == behind[common]:
            common += 1
        perform(ahead[:common])
        if len(ahead) > common:
            pl.when(z_lo == 3)(lambda: perform(ahead[common:]))
        if len(behind) > common:
            pl.when(z_lo < 3)(lambda: perform(behind[common:]))
        if work is not None:
            perform((work,))

    carry(0, sums[pl.ds(0, W)] + convolve(0, 2, 1))

    def unit_half(frame, half):
        return units.at[pl.ds(W * frame + W // 2 * half, W // 2)]

    def unit(h, convolved):
        units[pl.ds(W * (2 + h), W)] = (attended[h].astype(jnp.float32) + convolved).astype(jnp.bfloat16)
        for half in range(2):
            push(("unit", h, half), ("tm", 1), lambda half=half: (
                unit_half(2 + h, half), unit_half(h, half), frame_sems.at[4 + 2 * h + half]))

    def earlier_unit(h):
        for half in range(2):
            arrive(unit_half(h, half), frame_sems.at[4 + 2 * h + half])
        return earlier(units[pl.ds(W * h, W)])

    def put(h, stretched):
        out[2 * h] = stretched[:, :C]
        out[2 * h + 1] = stretched[:, C:]

    sums[...] = convolve(2, 2, 2)
    sums[pl.ds(W, W)] += convolve(1, 2, 1)
    unit(1, joined(sums[pl.ds(W, W)]) + brought(1))
    convolved = joined(sums[pl.ds(0, W)])
    last = dot(units[pl.ds(W * 3, W)], upsample[2])
    unit(0, convolved + brought(0))
    newest = units[pl.ds(W * 2, W)]
    last = last + dot(newest, upsample[1])
    first = dot(newest, upsample[2])
    newest = earlier_unit(1)
    put(1, last + dot(newest, upsample[0]))
    first = first + dot(newest, upsample[1])
    put(0, first + dot(earlier_unit(0), upsample[0]))
    for entry in sent.values():
        started(*entry).wait_send()


def body(latent_features, attn_gain, w_query, w_key, w_value, w_proj, unit_gain, conv_weight, upsample_weight):
    vmem = pl.BlockSpec(memory_space=pltpu.VMEM)
    hbm = pl.BlockSpec(memory_space=pltpu.HBM)
    bf16, f32 = jnp.bfloat16, jnp.float32
    out = pl.pallas_call(
        kernel,
        out_shape=jax.ShapeDtypeStruct((4, W, C), f32),
        in_specs=[hbm] * 9,
        out_specs=vmem,
        scratch_shapes=[
            pltpu.VMEM((2 * W, C), bf16),
            pltpu.VMEM((648, C), bf16),
            pltpu.VMEM((C,), f32),
            pltpu.VMEM((C,), f32),
            pltpu.VMEM((16, 2 * W, C), bf16),
            pltpu.VMEM((16, PART * PARTS, 128), bf16),
            pltpu.VMEM((PART * PARTS, 128), bf16),
            pltpu.VMEM((C, C), bf16),
            pltpu.VMEM((C, 2 * C), bf16),
            pltpu.VMEM((C, C), bf16),
            pltpu.VMEM((3, C, 2 * C), bf16),
            pltpu.VMEM((2, 2560, C), bf16),
            pltpu.VMEM((2, 2560, C + 128), bf16),
            pltpu.VMEM((2, 3 * W, C), bf16),
            pltpu.VMEM((2, 3 * W, C + 128), f32),
            pltpu.VMEM((2, 3 * W, 128), f32),
            pltpu.VMEM((2, W, C), bf16),
            pltpu.VMEM((2 * W, 3 * C), bf16),
            pltpu.VMEM((9 * C, 3 * C), bf16),
            pltpu.VMEM((2 * W, 3 * C), f32),
            pltpu.VMEM((4 * W, C), bf16),
            pltpu.VMEM((4 * W, C), bf16),
            pltpu.SemaphoreType.DMA((154,)),
            pltpu.SemaphoreType.DMA((96,)),
            pltpu.SemaphoreType.DMA((32,)),
            pltpu.SemaphoreType.DMA((32,)),
            pltpu.SemaphoreType.DMA((8,)),
            pltpu.SemaphoreType.DMA((11,)),
        ],
        compiler_params=pltpu.CompilerParams(
            collective_id=0, has_side_effects=True, vmem_limit_bytes=60 * 1024 * 1024),
    )(latent_features.reshape(2 * W, C), conv_weight.reshape(648, C), attn_gain, unit_gain,
      w_query, w_key, w_value, w_proj, upsample_weight)
    return out.astype(bf16).reshape(4, 1, W, C)


def solution(mesh):
    in_specs = (P("tm", "rows", None, None), P(), P(), P(), P(), P(), P(), P(None, None, None, "rows", None), P())
    return jax.shard_map(body, mesh=mesh, in_specs=in_specs, out_specs=P("tm", "rows", None, None), check_vma=False)
```
